128 devices in a mesh: blk: 32 (over y, x, core), ax: 4 (over z).
Axes of the slice: x: 4, y: 4, z: 4, core: 2. Of those that a mesh axis runs over, the one named last changes fastest.
Arguments:
- adjoint: bfloat16 [5, 32, 256, 64, 128], P(None, 'blk', 'ax'), may hold values from -6 to 6
- density: bfloat16 [32, 256, 64, 128], P('blk', 'ax'), may hold values from 0.5 to 1.5
- velocity: bfloat16 [3, 32, 256, 64, 128], P(None, 'blk', 'ax'), may hold values from -3 to 3
- pressure: bfloat16 [32, 256, 64, 128], P('blk', 'ax'), may hold values from 0.5 to 1.5
- metrics: bfloat16 [9, 32, 256, 64, 128], P(None, 'blk', 'ax'), may hold values from -6 to 6
- links: int32 [3, 32, 48], replicated, may hold values from -1 to 47, as said below
Outputs:
- rhs: bfloat16 [5, 32, 256, 64, 128], P(None, 'blk', 'ax')
The draws below stay inside these ranges and needn't reach their ends.
Inputs may be any that keep to these rules, and one draw needn't show every extreme that they name: links[0] is a source block or -1 (a physical boundary), links[1] a patch of that block, links[2] an orientation 0 or 1. No source patch is named twice. A block names at most 2 patches of any one source block, and some pair of blocks reaches exactly 2. The number of live patches differs between blocks, and at least one block has all 48 live.
All inputs are finite; a program needn't handle non-finite values.
Results may differ from the reference program's by a relative error of at most 0.001.
Values may be sent and summed in bfloat16 or wider, within the bound.
No kernel may reach another device: no remote copies, remote signals or barrier semaphores. Data moves between devices by JAX's collectives and lax.ppermute only.
A program may use at most 256 MiB of HBM per device.

```python
import jax
import jax.numpy as jnp
from jax import lax

NY = 64
NZ = 128
PW = 8
NX = 256
BLOCKS = 32
PATCHES = 48
CAPACITY = 2


def draw_links(key, part):
    subkeys = jax.random.split(key, 7)
    shift_count = PATCHES // CAPACITY
    block_order = jax.random.permutation(subkeys[0], BLOCKS)
    shifts = block_order[:shift_count]
    cycle_index = jnp.arange(PATCHES, dtype=jnp.int32) % shift_count
    slot_shift = shifts[cycle_index]
    slot_face = jax.random.permutation(subkeys[1], PATCHES)
    layout = jax.random.permutation(subkeys[2], BLOCKS)
    inverse_layout = jnp.zeros((BLOCKS,), jnp.int32).at[layout].set(jnp.arange(BLOCKS, dtype=jnp.int32))
    slot_keys = jax.random.split(subkeys[3], BLOCKS)
    slot_order = jax.vmap(lambda one_key: jax.random.permutation(one_key, PATCHES))(slot_keys)
    owner_block = jnp.arange(BLOCKS, dtype=jnp.int32)[:, None]
    source = inverse_layout[(layout[owner_block] + slot_shift[slot_order]) % BLOCKS]
    source_face = slot_face[slot_order]
    live_count = jax.random.randint(subkeys[4], (BLOCKS,), PATCHES // 4, PATCHES + 1)
    full_block = jax.random.randint(subkeys[5], (), 0, BLOCKS)
    live_count = live_count.at[full_block].set(PATCHES)
    active = slot_order < live_count[:, None]
    reversed_flag = jax.random.randint(subkeys[6], (BLOCKS, PATCHES), 0, 2)
    source = jnp.where(active, source, -1)
    return jnp.stack([source, source_face, reversed_flag]).astype(jnp.int32)


def hump_profile(count, periods):
    position = (jnp.arange(count, dtype=jnp.float32) + 0.5) / count
    return jnp.sin(jnp.pi * periods * position)


def draw_adjoint(key, part):
    subkeys = jax.random.split(jax.random.fold_in(key, 917), 4)
    full_shape = (5, BLOCKS, NX, NY, NZ)
    level = jax.random.uniform(subkeys[0], (5,), jnp.float32, 3.0, 4.5)
    second_periods = 2.0
    noise = 0.1 * jax.random.truncated_normal(subkeys[2], -4.0, 4.0, full_shape, jnp.float32)
    sign_pick = jax.random.randint(subkeys[1], (5,), 0, 2)
    signed_level = level * (2.0 * sign_pick.astype(jnp.float32) - 1.0)
    second_level = jax.random.uniform(subkeys[3], (5, BLOCKS), jnp.float32, -0.5, 0.5)
    axial_main = hump_profile(NX, 1.0)
    axial_second = hump_profile(NX, second_periods)
    lateral = hump_profile(NY, 1.0)[:, None] * hump_profile(NZ, 1.0)[None, :]
    axial = signed_level[:, None, None] * axial_main[None, None, :] + second_level[:, :, None] * axial_second[None, None, :]
    smooth = axial[:, :, :, None, None] * lateral[None, None, None, :, :]
    return (smooth + noise).astype(jnp.bfloat16)


def levels(own_key, extent, cuts, low, high):
    def one(dim, parts):
        draws = jax.random.uniform(jax.random.fold_in(jax.random.fold_in(own_key, 6), dim), (parts,), jnp.float32, low / len(cuts), high / len(cuts))
        return jnp.repeat(jnp.exp(draws), extent[dim] // parts).reshape((-1,) + (1,) * (len(extent) - dim - 1))

    loudness = one(*cuts[0])
    for cut in cuts[1:]:
        loudness = loudness * one(*cut)
    return loudness


def centred(stream_key, shape, scale, bound, cuts=(), held_as=jnp.bfloat16):
    drawn = scale * jax.random.normal(stream_key, shape, jnp.float32)
    if cuts:
        drawn = drawn * levels(stream_key, shape, cuts, -0.22, 0.18)
    return jnp.clip(drawn, -bound, bound).astype(held_as)


def setup_inputs(seed: int = 0) -> dict:
    keys = jax.random.split(jax.random.key(seed), 7)
    return {
        "adjoint": draw_adjoint(jax.random.fold_in(keys[6], 71), 0),
        "density": jnp.clip(0.5 + 1.0 * jax.random.uniform(keys[1], (BLOCKS, NX, NY, NZ), jnp.float32) ** levels(keys[1], (BLOCKS, NX, NY, NZ), ((0, 32), (1, 4)), -0.2, 0.2), 0.5, 1.5).astype(jnp.bfloat16),
        "velocity": centred(keys[2], (3, BLOCKS, NX, NY, NZ), 0.5, 3.0, ((1, 32), (2, 4))),
        "pressure": jnp.clip(0.5 + 1.0 * jax.random.uniform(keys[3], (BLOCKS, NX, NY, NZ), jnp.float32) ** levels(keys[3], (BLOCKS, NX, NY, NZ), ((0, 32), (1, 4)), -0.2, 0.2), 0.5, 1.5).astype(jnp.bfloat16),
        "metrics": centred(keys[4], (9, BLOCKS, NX, NY, NZ), 1.0, 6.0, ((1, 32), (2, 4))),
        "links": draw_links(jax.random.fold_in(keys[6], 71), 0),
    }


lhs_alpha = 1.0 / 3.0
near_coef = 7.0 / 9.0
far_coef = 1.0 / 36.0
heat_ratio = 1.4
penalty_weight = 1.0

def line_tables(line_cells):
    position = jnp.arange(line_cells, dtype=jnp.int32)
    middle = jnp.ones((line_cells,), jnp.float32)
    sub_diag = jnp.where(position > 0, lhs_alpha, 0.0).astype(jnp.float32)
    super_diag = jnp.where(position < line_cells - 1, lhs_alpha, 0.0).astype(jnp.float32)
    offset = position[None, :] - position[:, None]
    stencil = near_coef * ((offset == 1).astype(jnp.float32) - (offset == -1).astype(jnp.float32))
    stencil = stencil + far_coef * ((offset == 2).astype(jnp.float32) - (offset == -2).astype(jnp.float32))
    inverse = lax.linalg.tridiagonal_solve(sub_diag, middle, super_diag, jnp.eye(line_cells, dtype=jnp.float32))
    derivative = lax.linalg.tridiagonal_solve(sub_diag, middle, super_diag, stencil)
    return (inverse, derivative)

def flux_terms(gradient, metric, density, velocity, pressure):
    contravariant = metric[0] * velocity[0] + metric[1] * velocity[1] + metric[2] * velocity[2]
    coupled = density * gradient[0] + heat_ratio * pressure * gradient[4]
    turned = (metric[0] * gradient[1] + metric[1] * gradient[2] + metric[2] * gradient[3]) / density
    return jnp.stack([contravariant * gradient[0], contravariant * gradient[1] + metric[0] * coupled, contravariant * gradient[2] + metric[1] * coupled, contravariant * gradient[3] + metric[2] * coupled, contravariant * gradient[4] + turned])

def face_patches(source_field):
    pieces = []
    for surface in (source_field[:, :, 0, :], source_field[:, :, -1, :], source_field[:, :, :, 0], source_field[:, :, :, -1]):
        fields, row_count, length = surface.shape
        grouped = surface.reshape(fields, row_count, length // PW, PW)
        pieces.append(jnp.transpose(grouped, (2, 0, 1, 3)))
    return jnp.concatenate(pieces, axis=0)

def add_patches(running, penalty):
    fields, row_count, y_count, z_count = running.shape
    z_parts = z_count // PW
    y_parts = y_count // PW

    def unfold(stacked, length):
        return jnp.transpose(stacked, (1, 2, 0, 3)).reshape(fields, row_count, length)
    running = running.at[:, :, 0, :].add(unfold(penalty[:z_parts], z_count))
    running = running.at[:, :, -1, :].add(unfold(penalty[z_parts:2 * z_parts], z_count))
    running = running.at[:, :, :, 0].add(unfold(penalty[2 * z_parts:2 * z_parts + y_parts], y_count))
    running = running.at[:, :, :, -1].add(unfold(penalty[2 * z_parts + y_parts:], y_count))
    return running

def reference(adjoint, density, velocity, pressure, metrics, links):
    highest = lax.Precision.HIGHEST
    axial_table = line_tables(NX)[1]
    cross_table = line_tables(NY)[1]
    depth_table = line_tables(NZ)[1]
    all_faces = jax.vmap(face_patches, in_axes=1)(adjoint)

    def one_block(block_id):
        block_field = lax.dynamic_index_in_dim(adjoint, block_id, 1, keepdims=False).astype(jnp.float32)
        density_f = lax.dynamic_index_in_dim(density, block_id, 0, keepdims=False).astype(jnp.float32)
        velocity_f = lax.dynamic_index_in_dim(velocity, block_id, 1, keepdims=False).astype(jnp.float32)
        pressure_f = lax.dynamic_index_in_dim(pressure, block_id, 0, keepdims=False).astype(jnp.float32)
        metric_f = lax.dynamic_index_in_dim(metrics, block_id, 1, keepdims=False).astype(jnp.float32)
        grad_x = jnp.einsum('ij,fjyz->fiyz', axial_table, block_field, precision=highest)
        grad_y = jnp.einsum('ij,fxjz->fxiz', cross_table, block_field, precision=highest)
        grad_z = jnp.einsum('ij,fxyj->fxyi', depth_table, block_field, precision=highest)
        flux_sum = flux_terms(grad_x, metric_f[0:3], density_f, velocity_f, pressure_f)
        flux_sum = flux_sum + flux_terms(grad_y, metric_f[3:6], density_f, velocity_f, pressure_f)
        flux_sum = flux_sum + flux_terms(grad_z, metric_f[6:9], density_f, velocity_f, pressure_f)
        own_faces = face_patches(block_field)
        own_links = lax.dynamic_index_in_dim(links, block_id, 1, keepdims=False)
        source = own_links[0]
        source_face = own_links[1]
        reversed_flag = own_links[2]
        neighbour = all_faces[jnp.maximum(source, 0), source_face].astype(jnp.float32)
        neighbour = jnp.where((reversed_flag == 1)[:, None, None, None], neighbour[..., ::-1], neighbour)
        penalty = jnp.where((source >= 0)[:, None, None, None], penalty_weight * (neighbour - own_faces), 0.0)
        return add_patches(flux_sum, penalty).astype(jnp.bfloat16)
    result = lax.map(one_block, jnp.arange(BLOCKS, dtype=jnp.int32))
    return jnp.transpose(result, (1, 0, 2, 3, 4))
```

```python
import functools

import jax
import jax.numpy as jnp
import numpy as np
from jax import lax
from jax.experimental import pallas as pl
from jax.experimental.pallas import tpu as pltpu
from jax.sharding import PartitionSpec as P

PW = 8
ALPHA = 1.0 / 3.0
NEAR = 7.0 / 9.0
FAR = 1.0 / 36.0
HEAT = 1.4
PIVOT = (1.0 + np.sqrt(1.0 - 4.0 * ALPHA * ALPHA)) / 2.0
MULT = ALPHA / PIVOT
F32 = jnp.float32
BF16 = jnp.bfloat16
MIB = 1 << 20


def dense(n):
    eye = functools.partial(np.eye, n)
    left = eye() + ALPHA * (eye(k=1) + eye(k=-1))
    right = NEAR * (eye(k=1) - eye(k=-1)) + FAR * (eye(k=2) - eye(k=-2))
    return left, right


def split(table):
    high = table.astype(np.float32).astype(jnp.bfloat16)
    low = (table - high.astype(np.float64)).astype(jnp.bfloat16)
    return high, low


def lateral_tables(ny, nz):
    left, right = dense(ny)
    high, low = split(np.linalg.solve(left, right))
    along_y = np.concatenate([high, low], axis=1)
    left, right = dense(nz)
    high, low = split(np.linalg.solve(left, right).T)
    along_z = np.concatenate([high, low], axis=0)
    return along_y, along_z


def axial_tables(pieces, length):
    n = pieces * length
    left, right = dense(n)
    derivative = np.linalg.solve(left, right)
    rows = [np.arange(s * length, (s + 1) * length) for s in range(pieces)]
    edge = []
    for s in range(pieces):
        shifted = right[rows[s]].copy()
        for other in (np.arange(0, s * length), np.arange((s + 1) * length, n)):
            if other.size:
                gain = left[np.ix_(rows[s], other)] @ np.linalg.inv(left[np.ix_(other, other)])
                shifted -= gain @ right[other]
        edge.append(shifted)
    weights = np.zeros((pieces, 2 * length))
    scalars = np.zeros((pieces, 16))
    for s in range(pieces):
        own = rows[s]
        if s + 1 < pieces:
            weights[s, :length] = edge[s + 1][0, own]
        if s > 0:
            weights[s, length:] = edge[s - 1][-1, own]
        else:
            weights[s, length:] = -(1.0 - PIVOT) * derivative[0, own]
    unit = abs(edge[2][0, rows[0][-1]])
    for s in range(pieces):
        own = rows[s]
        if s + 2 < pieces:
            vector = edge[s + 2][0, own] / unit
            scalars[s, 0] = vector[0] / weights[s, 0]
            scalars[s, 2] = vector[-1] - scalars[s, 0] * weights[s, length - 1]
            rest = vector - scalars[s, 0] * weights[s, :length]
            rest[-1] = 0.0
        else:
            vector = edge[s - 2][-1, own] / unit
            scalars[s, 1] = vector[-1] / weights[s, -1]
            scalars[s, 3] = vector[0] - scalars[s, 1] * weights[s, length]
            rest = vector - scalars[s, 1] * weights[s, length:]
            rest[0] = 0.0
        assert np.abs(rest).max() < 1e-12
        if s > 0:
            scalars[s, 4] = edge[s][0, own[0]]
            scalars[s, 5] = edge[s][0, own[1]] - NEAR
        else:
            scalars[s, 6] = 1.0
            vector = -(1.0 - PIVOT) * derivative[0, rows[1]]
            scalars[s, 7] = vector[-1] / weights[1, -1]
            scalars[s, 8] = vector[0] - scalars[s, 7] * weights[1, length]
        if s + 1 < pieces:
            scalars[s, 9] = edge[s][-1, own[-1]]
            scalars[s, 10] = edge[s][-1, own[-2]] + NEAR
        scalars[s, 11] = unit if s >= 2 else 0.0
        scalars[s, 12] = unit if s < 2 else 0.0
        last = PIVOT - ALPHA * ALPHA / PIVOT if s + 1 < pieces else PIVOT
        scalars[s, 13] = (1.0 - PIVOT / last) / MULT
    return np.concatenate([weights, scalars], axis=1).astype(np.float32)


def lane_order():
    table = np.zeros((256, 256), np.float32)
    for pair in range(2):
        for x in range(64):
            table[128 * pair + 2 * x, 64 * pair + x] = 1.0
            table[128 * pair + (2 * x - 1) % 128, 128 + 64 * pair + x] = 1.0
    return table.astype(jnp.bfloat16)


def dot(a, b):
    return jnp.dot(a, b, preferred_element_type=F32)


def dot_nt(a, b):
    return lax.dot_general(a, b, (((1,), (1,)), ((), ())), preferred_element_type=F32)


def iota(shape, axis):
    return lax.broadcasted_iota(jnp.int32, shape, axis)


def split_two(value):
    high = value.astype(BF16)
    return high, (value - high.astype(F32)).astype(BF16)


def gather_kernel(
    fields, table, links, order, f_ref, send, right, left, far, face_y, face_z, keep_y, keep_z
):
    step = pl.program_id(0)
    place = lax.axis_index("ax")
    nx, ny, nz = f_ref.shape[2:]
    lane = iota((ny, nz), 1)

    def group(g, carry):
        to_right, to_left, columns = carry
        part = jnp.zeros((ny, nz), F32)
        for j in range(8):
            x = 8 * g + j
            tile = f_ref[0, 0, x].astype(F32)
            to_right = to_right + table[place, x] * tile
            to_left = to_left + table[place, nx + x] * tile
            turned = pltpu.roll(tile, 2 * j, 1) if j else tile
            part = jnp.where(((lane + 1 - 2 * j) & 127) < 2, turned, part)
        part = pltpu.roll(part, 16 * g, 1)
        columns = jnp.where(((lane + 1 - 16 * g) & 127) < 16, part, columns)
        return to_right, to_left, columns

    zero = jnp.zeros((ny, nz), F32)
    to_right, to_left, columns = lax.fori_loop(0, nx // 8, group, (zero, zero, zero))
    first = f_ref[0, 0, 0]
    last = f_ref[0, 0, nx - 1]
    right[0, 0] = last
    right[0, 1], right[0, 2] = split_two(to_right)
    left[0, 0] = first
    left[0, 1], left[0, 2] = split_two(to_left)
    base = 2 * nx
    far[0] = (
        table[place, base] * to_right
        + table[place, base + 1] * to_left
        + table[place, base + 2] * last.astype(F32)
        + table[place, base + 3] * first.astype(F32)
    ).astype(BF16)
    columns = columns.astype(BF16)
    face_z[0] = columns
    keep_z[step] = columns
    pick = iota((nx, 16 * nx), 1) - 16 * iota((nx, 16 * nx), 0)
    low = dot((pick == 0).astype(F32).astype(BF16), f_ref[0, 0, :, 0:16, :].reshape(16 * nx, nz))
    high = dot(
        (pick == 15).astype(F32).astype(BF16), f_ref[0, 0, :, ny - 16 : ny, :].reshape(16 * nx, nz)
    )
    faces = jnp.concatenate([low, high], axis=1).astype(BF16)
    face_y[0] = faces
    keep_y[step] = faces

    @pl.when(step == fields - 1)
    def _():
        own = lax.axis_index("blk")
        source = links[0]
        blocks, patches = source.shape
        hit = (source == own).astype(F32)
        before = (iota((patches, patches), 0) < iota((patches, patches), 1)).astype(F32)
        rank = dot(hit.astype(BF16), before.astype(BF16))
        face = links[1].astype(F32) + 1.0
        columns = []
        for c in range(2):
            chosen = jnp.where(rank == float(c), hit, 0.0) * face
            chosen = jnp.sum(chosen, axis=1, keepdims=True)
            columns.append(jnp.broadcast_to(chosen, (blocks, 128)))
        chosen = jnp.concatenate(columns, axis=0).astype(BF16)
        rows = 16 * blocks
        row = iota((rows, 2 * blocks), 0)
        slot = (row & 15) // 8 * blocks + row // 16
        spread = (slot == iota((rows, 2 * blocks), 1)).astype(F32).astype(BF16)
        chosen = dot(spread, chosen)
        cells = PW * patches
        target = (chosen.astype(jnp.int32) - 1) * PW + (iota((rows, 128), 0) & 7)
        target = jnp.concatenate([target] * (cells // 128), axis=1)
        chooser = (iota((rows, cells), 1) == target).astype(F32).astype(BF16)
        for pair in range((fields + 1) // 2):
            one = 2 * pair
            if one + 1 < fields:
                ys = jnp.concatenate([keep_y[one], keep_y[one + 1]], axis=0)
                zs = jnp.concatenate([keep_z[one], keep_z[one + 1]], axis=1)
            else:
                ys = jnp.concatenate([keep_y[one], jnp.zeros_like(keep_y[one])], axis=0)
                zs = jnp.concatenate([keep_z[one], jnp.zeros_like(keep_z[one])], axis=1)
            zs = dot(zs, order[...]).astype(BF16)
            zs = jnp.concatenate([zs[:, :128], zs[:, 128:]], axis=0)
            out = dot_nt(chooser[:, : 2 * nz], ys) + dot(chooser[:, 2 * nz :], zs)
            send[:, :, 128 * pair : 128 * pair + 128] = out.astype(BF16).reshape(blocks, 16, 128)


def flux(gradients, metric, density, velocity, pressure, sums):
    ka, kb, kc = metric
    speed = ka * velocity[0] + kb * velocity[1] + kc * velocity[2]
    coupled = density * gradients[0] + pressure * gradients[4]
    turned = ka * gradients[1] + kb * gradients[2] + kc * gradients[3]
    terms = [
        speed * gradients[0],
        speed * gradients[1] + ka * coupled,
        speed * gradients[2] + kb * coupled,
        speed * gradients[3] + kc * coupled,
        speed * gradients[4],
        turned,
    ]
    return terms if sums is None else [a + b for a, b in zip(sums, terms)]


def lateral_kernel(fields, along_y, along_z, f_ref, density, velocity, pressure, ky, kz, out):
    chunk, ny, nz = f_ref.shape[2:]

    def body(h, _):
        grads_y = []
        grads_z = []
        xs = (2 * h, 2 * h + 1)
        for f in range(fields):
            tiles = [f_ref[f, 0, x] for x in xs]
            rows = jnp.concatenate(tiles, axis=0)
            grads_z.append(dot(jnp.concatenate([rows, rows], axis=1), along_z[...]))
            wide = jnp.concatenate(tiles, axis=1)
            grads_y.append(dot(along_y[...], jnp.concatenate([wide, wide], axis=0)))
        for q, x in enumerate(xs):
            for y in range(0, ny, 16):
                at = slice(y, y + 16)
                rho = density[0, x, at, :].astype(F32)
                vel = [velocity[i, 0, x, at, :].astype(F32) for i in range(3)]
                press = HEAT * pressure[0, x, at, :].astype(F32)
                gy = [g[at, q * nz : (q + 1) * nz] for g in grads_y]
                gz = [g[q * ny + y : q * ny + y + 16] for g in grads_z]
                metric = [ky[i, 0, x, at, :].astype(F32) for i in range(3)]
                sums = flux(gy, metric, rho, vel, press, None)
                metric = [kz[i, 0, x, at, :].astype(F32) for i in range(3)]
                sums = flux(gz, metric, rho, vel, press, sums)
                for i in range(4):
                    out[i, x, at, :] = sums[i]
                out[4, x, at, :] = sums[4] + sums[5] / rho
        return 0

    lax.fori_loop(0, chunk // 2, body, 0)


def axial_kernel(
    fields,
    table,
    links,
    order,
    f_ref,
    density,
    velocity,
    pressure,
    kx,
    partial,
    received,
    right,
    left,
    far,
    own_left,
    face_y,
    face_z,
    out,
    line,
    pen_y,
    pen_z,
):
    step = pl.program_id(0)
    place = lax.axis_index("ax")
    nx, rows, nz = f_ref.shape[2:]
    ny = face_z.shape[1]

    @pl.when(step == 0)
    def _():
        own = lax.axis_index("blk")
        blocks, patches = links.shape[1:]
        cells = PW * patches
        source = links[0, pl.ds(own, 1), :]
        turn = links[2, pl.ds(own, 1), :]
        same = (patches, patches)
        wide = jnp.broadcast_to(source, same).astype(F32)
        tall = jnp.sum(
            jnp.where(iota(same, 0) == iota(same, 1), wide, 0.0), axis=1, keepdims=True
        )
        earlier = (iota(same, 0) < iota(same, 1)) & (wide == tall)
        slot = jnp.sum(earlier.astype(F32), axis=0, keepdims=True)
        live = (source >= 0).astype(F32)
        where = jnp.where(source >= 0, source.astype(F32) * 16.0 + slot * 8.0, -16.0)
        shape = (cells, patches)
        mine = (iota(shape, 0) // PW) == iota(shape, 1)

        def spread(value):
            value = jnp.where(mine, jnp.broadcast_to(value, shape), 0.0)
            return jnp.sum(value, axis=1, keepdims=True)

        cell = iota((cells, 1), 0) & 7
        cell = jnp.where(spread(turn.astype(F32)) > 0.5, 7 - cell, cell)
        target = spread(where).astype(jnp.int32) + cell
        slots = 16 * blocks
        chooser = (iota((cells, slots), 1) == target).astype(F32).astype(BF16)
        live_rows = spread(live)
        got = dot(chooser, received[...].reshape(slots, received.shape[2]))
        got_y = jnp.transpose(got[: 2 * nz])
        across = jnp.sum(
            jnp.where(
                iota((patches, 2 * nz), 0) == iota((patches, 2 * nz), 1) // PW,
                jnp.broadcast_to(
                    jnp.sum(
                        jnp.where(
                            iota(same, 0) == iota(same, 1), jnp.broadcast_to(live, same), 0.0
                        ),
                        axis=1,
                        keepdims=True,
                    ),
                    (patches, 2 * nz),
                ),
                0.0,
            ),
            axis=0,
            keepdims=True,
        )
        for f in range(fields):
            value = got_y[nx * f : nx * f + nx] - across * face_y[f].astype(F32)
            pen_y[0, nx * f : nx * f + nx, :] = value[:, :nz]
            pen_y[1, nx * f : nx * f + nx, :] = value[:, nz:]
        even = (iota((ny, 128), 1) & 1) == 0
        live_z = jnp.where(
            even, live_rows[2 * nz : 2 * nz + ny], live_rows[2 * nz + ny : 2 * nz + 2 * ny]
        )
        for pair in range((fields + 1) // 2):
            lanes = slice(128 * pair, 128 * pair + 128)
            both = jnp.concatenate(
                [got[2 * nz : 2 * nz + ny, lanes], got[2 * nz + ny :, lanes]], axis=1
            )
            both = dot_nt(both.astype(BF16), order[...])
            for q in range(2):
                f = 2 * pair + q
                if f < fields:
                    pen_z[f] = both[:, 128 * q : 128 * q + 128] - live_z * face_z[f].astype(F32)

    base = 2 * nx

    def scalar(i):
        return table[place, base + i]

    inverse = 1.0 / PIVOT
    near = NEAR * inverse
    far_coef = FAR * inverse

    def load(f, x):
        return f_ref[f, 0, x].astype(F32)

    def edges(f):
        right_fn = right[f, 1].astype(F32) + right[f, 2].astype(F32)
        left_fn = left[f, 1].astype(F32) + left[f, 2].astype(F32)
        own_fn = own_left[f, 1].astype(F32) + own_left[f, 2].astype(F32)
        right_last = right[f, 0].astype(F32)
        left_first = left[f, 0].astype(F32)
        far_plane = far[f].astype(F32)
        low = (
            right_fn
            + scalar(4) * load(f, 0)
            + scalar(5) * load(f, 1)
            + scalar(6) * own_fn
            + scalar(7) * left_fn
            + scalar(8) * left_first
            + scalar(11) * far_plane
        )
        high = (
            left_fn
            + scalar(9) * load(f, nx - 1)
            + scalar(10) * load(f, nx - 2)
            + scalar(12) * far_plane
        )
        return (
            low * inverse,
            -far_coef * right_last,
            far_coef * left_first,
            high * inverse,
        )

    for members in ((0, 1, 2), (3, 4)):
        edge = [edges(f) for f in members]
        state = []
        for q, f in enumerate(members):
            f0, f1, f2, f3 = [load(f, x) for x in range(4)]
            d0 = near * f1 + far_coef * f2 + edge[q][0]
            d1 = near * (f2 - f0) + far_coef * f3 + edge[q][1] - MULT * d0
            line[0, f] = d0
            line[1, f] = d1
            state.append((f0, f1, f2, f3, d1))

        def forward(x, state):
            new = []
            for q, f in enumerate(members):
                fm2, fm1, f0, fp1, d = state[q]
                fp2 = load(f, x + 2)
                d = (near * (fp1 - fm1) + far_coef * (fp2 - fm2)) - MULT * d
                line[x, f] = d
                new.append((fm1, f0, fp1, fp2, d))
            return tuple(new)

        state = lax.fori_loop(2, nx - 2, forward, tuple(state), unroll=4)
        for q, f in enumerate(members):
            fm2, fm1, f0, fp1, d = state[q]
            d = near * (fp1 - fm1) - far_coef * fm2 + edge[q][2] - MULT * d
            line[nx - 2, f] = d
            d = -near * f0 - far_coef * fm1 + edge[q][3] - MULT * d
            line[nx - 1, f] = d

    lane = iota((rows, nz), 1)
    at_z = ((lane + 1) & 127) < 2
    row = iota((rows, nz), 0)
    last_step = pl.num_programs(0) - 1
    at_y = ((row == 0) & (step == 0)) | ((row == rows - 1) & (step == last_step))
    side = (step == last_step).astype(jnp.int32)
    y_at = pl.multiple_of(step * rows, rows)

    def backward(k, g):
        x = nx - 1 - k
        g = [line[x, f] - MULT * g[f] for f in range(fields)]
        rho = density[0, x].astype(F32)
        vel = [velocity[i, 0, x].astype(F32) for i in range(3)]
        press = HEAT * pressure[0, x].astype(F32)
        metric = [kx[i, 0, x].astype(F32) for i in range(3)]
        sums = flux(g, metric, rho, vel, press, None)
        sums[4] = sums[4] + sums[5] / rho
        for f in range(fields):
            total = sums[f] + partial[f, x]
            total = total + jnp.where(at_y, pen_y[side, pl.ds(f * nx + x, 1), :], 0.0)
            turned = pltpu.roll(pen_z[f, pl.ds(y_at, rows), :], (128 - 2 * x) & 127, 1)
            total = total + jnp.where(at_z, turned, 0.0)
            out[f, 0, x] = total.astype(BF16)
        return g

    start = [scalar(13) * line[nx - 1, f] for f in range(fields)]
    lax.fori_loop(0, nx, backward, start, unroll=2)


def in_hbm(*arrays):
    return [pltpu.with_memory_space_constraint(a, pltpu.HBM) for a in arrays]


def whole(shape):
    return pl.BlockSpec(shape, lambda *_: (0,) * len(shape))


def body(tables, adjoint, density, velocity, pressure, metrics, links):
    fields, _, nx, ny, nz = adjoint.shape
    blocks, patches = links.shape[1:]
    along_y, along_z, axial, order = [jnp.asarray(t) for t in tables]
    smem = pl.BlockSpec(memory_space=pltpu.SMEM)
    lanes = 128 * ((fields + 1) // 2)
    shape = jax.ShapeDtypeStruct
    send, right, left, far, face_y, face_z = pl.pallas_call(
        functools.partial(gather_kernel, fields),
        grid=(fields,),
        in_specs=[
            smem,
            whole(links.shape),
            whole(order.shape),
            pl.BlockSpec((1, 1, nx, ny, nz), lambda i: (i, 0, 0, 0, 0)),
        ],
        out_specs=[
            whole((blocks, 16, lanes)),
            pl.BlockSpec((1, 3, ny, nz), lambda i: (i, 0, 0, 0)),
            pl.BlockSpec((1, 3, ny, nz), lambda i: (i, 0, 0, 0)),
            pl.BlockSpec((1, ny, nz), lambda i: (i, 0, 0)),
            pl.BlockSpec((1, nx, 2 * nz), lambda i: (i, 0, 0)),
            pl.BlockSpec((1, ny, 128), lambda i: (i, 0, 0)),
        ],
        out_shape=[
            shape((blocks, 16, lanes), BF16),
            shape((fields, 3, ny, nz), BF16),
            shape((fields, 3, ny, nz), BF16),
            shape((fields, ny, nz), BF16),
            shape((fields, nx, 2 * nz), BF16),
            shape((fields, ny, 128), BF16),
        ],
        scratch_shapes=[
            pltpu.VMEM((fields, nx, 2 * nz), BF16),
            pltpu.VMEM((fields, ny, 128), BF16),
        ],
        compiler_params=pltpu.CompilerParams(vmem_limit_bytes=16 * MIB),
        cost_estimate=pl.CostEstimate(flops=10**9, bytes_accessed=7 * 10**6, transcendentals=0),
    )(axial, *in_hbm(links, order, adjoint))
    received = lax.all_to_all(send, "blk", 0, 0)
    pieces = lax.axis_size("ax")
    from_left = lax.ppermute(right, "ax", [(i, i + 1) for i in range(pieces - 1)])
    from_right = lax.ppermute(left, "ax", [(i + 1, i) for i in range(pieces - 1)])
    from_far = lax.ppermute(far, "ax", [(i, (i + 2) % pieces) for i in range(pieces)])

    chunk = 8
    flow = [
        pl.BlockSpec((fields, 1, chunk, ny, nz), lambda i: (0, 0, i, 0, 0)),
        pl.BlockSpec((1, chunk, ny, nz), lambda i: (0, i, 0, 0)),
        pl.BlockSpec((3, 1, chunk, ny, nz), lambda i: (0, 0, i, 0, 0)),
        pl.BlockSpec((1, chunk, ny, nz), lambda i: (0, i, 0, 0)),
    ]
    partial = pl.pallas_call(
        functools.partial(lateral_kernel, fields),
        grid=(nx // chunk,),
        in_specs=[whole(along_y.shape), whole(along_z.shape)]
        + flow
        + [
            pl.BlockSpec((3, 1, chunk, ny, nz), lambda i: (1, 0, i, 0, 0)),
            pl.BlockSpec((3, 1, chunk, ny, nz), lambda i: (2, 0, i, 0, 0)),
        ],
        out_specs=pl.BlockSpec((fields, chunk, ny, nz), lambda i: (0, i, 0, 0)),
        out_shape=pltpu.VMEM((fields, nx, ny, nz), F32),
        compiler_params=pltpu.CompilerParams(vmem_limit_bytes=16 * MIB),
        cost_estimate=pl.CostEstimate(
            flops=10**10, bytes_accessed=27 * 10**6, transcendentals=0
        ),
    )(*in_hbm(along_y, along_z, adjoint, density, velocity, pressure, metrics, metrics))

    rows = 16
    return pl.pallas_call(
        functools.partial(axial_kernel, fields),
        grid=(ny // rows,),
        in_specs=[
            smem,
            whole(links.shape),
            whole(order.shape),
            pl.BlockSpec((fields, 1, nx, rows, nz), lambda i: (0, 0, 0, i, 0)),
            pl.BlockSpec((1, nx, rows, nz), lambda i: (0, 0, i, 0)),
            pl.BlockSpec((3, 1, nx, rows, nz), lambda i: (0, 0, 0, i, 0)),
            pl.BlockSpec((1, nx, rows, nz), lambda i: (0, 0, i, 0)),
            pl.BlockSpec((3, 1, nx, rows, nz), lambda i: (0, 0, 0, i, 0)),
            pl.BlockSpec((fields, nx, rows, nz), lambda i: (0, 0, i, 0)),
            whole(received.shape),
            pl.BlockSpec((fields, 3, rows, nz), lambda i: (0, 0, i, 0)),
            pl.BlockSpec((fields, 3, rows, nz), lambda i: (0, 0, i, 0)),
            pl.BlockSpec((fields, rows, nz), lambda i: (0, i, 0)),
            pl.BlockSpec((fields, 3, rows, nz), lambda i: (0, 0, i, 0)),
            whole(face_y.shape),
            whole(face_z.shape),
        ],
        out_specs=pl.BlockSpec((fields, 1, nx, rows, nz), lambda i: (0, 0, 0, i, 0)),
        out_shape=shape(adjoint.shape, BF16),
        scratch_shapes=[
            pltpu.VMEM((nx, fields, rows, nz), F32),
            pltpu.VMEM((2, fields * nx, nz), F32),
            pltpu.VMEM((fields, ny, 128), F32),
        ],
        compiler_params=pltpu.CompilerParams(vmem_limit_bytes=30 * MIB),
        cost_estimate=pl.CostEstimate(
            flops=10**10, bytes_accessed=30 * 10**6, transcendentals=0
        ),
    )(
        axial,
        *in_hbm(links, order, adjoint, density, velocity, pressure, metrics),
        pltpu.with_memory_space_constraint(partial, pltpu.VMEM),
        *in_hbm(received, from_left, from_right, from_far, left, face_y, face_z),
    )


def solution(mesh):
    in_specs = (
        P(None, "blk", "ax", None, None),
        P("blk", "ax", None, None),
        P(None, "blk", "ax", None, None),
        P("blk", "ax", None, None),
        P(None, "blk", "ax", None, None),
        P(),
    )
    out_specs = P(None, "blk", "ax", None, None)

    def run(*args):
        pieces = mesh.shape["ax"]
        nx, ny, nz = args[0].shape[2:]
        tables = (*lateral_tables(ny, nz), axial_tables(pieces, nx // pieces), lane_order())
        return jax.shard_map(
            functools.partial(body, tables),
            mesh=mesh,
            in_specs=in_specs,
            out_specs=out_specs,
            check_vma=False,
        )(*args)

    return run
```

```python
import functools

import jax
import jax.numpy as jnp
import numpy as np
from jax import lax
from jax.experimental import pallas as pl
from jax.experimental.pallas import tpu as pltpu
from jax.sharding import PartitionSpec as P

PW = 8
ALPHA = 1.0 / 3.0
NEAR = 7.0 / 9.0
FAR = 1.0 / 36.0
HEAT = 1.4
PIVOT = (1.0 + np.sqrt(1.0 - 4.0 * ALPHA * ALPHA)) / 2.0
MULT = ALPHA / PIVOT
F32 = jnp.float32
BF16 = jnp.bfloat16
MIB = 1 << 20


def dense(n):
    eye = functools.partial(np.eye, n)
    left = eye() + ALPHA * (eye(k=1) + eye(k=-1))
    right = NEAR * (eye(k=1) - eye(k=-1)) + FAR * (eye(k=2) - eye(k=-2))
    return left, right


def split(table):
    high = table.astype(np.float32).astype(jnp.bfloat16)
    low = (table - high.astype(np.float64)).astype(jnp.bfloat16)
    return high, low


def lateral_tables(ny, nz):
    left, right = dense(ny)
    high, low = split(np.linalg.solve(left, right))
    along_y = np.concatenate([high, low], axis=1)
    left, right = dense(nz)
    high, low = split(np.linalg.solve(left, right).T)
    along_z = np.concatenate([high, low], axis=0)
    return along_y, along_z


def axial_tables(pieces, length):
    n = pieces * length
    left, right = dense(n)
    derivative = np.linalg.solve(left, right)
    rows = [np.arange(s * length, (s + 1) * length) for s in range(pieces)]
    edge = []
    for s in range(pieces):
        shifted = right[rows[s]].copy()
        for other in (np.arange(0, s * length), np.arange((s + 1) * length, n)):
            if other.size:
                gain = left[np.ix_(rows[s], other)] @ np.linalg.inv(left[np.ix_(other, other)])
                shifted -= gain @ right[other]
        edge.append(shifted)
    weights = np.zeros((pieces, 2 * length))
    scalars = np.zeros((pieces, 16))
    for s in range(pieces):
        own = rows[s]
        if s + 1 < pieces:
            weights[s, :length] = edge[s + 1][0, own]
        if s > 0:
            weights[s, length:] = edge[s - 1][-1, own]
        else:
            weights[s, length:] = -(1.0 - PIVOT) * derivative[0, own]
    unit = abs(edge[2][0, rows[0][-1]])
    for s in range(pieces):
        own = rows[s]
        if s + 2 < pieces:
            vector = edge[s + 2][0, own] / unit
            scalars[s, 0] = vector[0] / weights[s, 0]
            scalars[s, 2] = vector[-1] - scalars[s, 0] * weights[s, length - 1]
            rest = vector - scalars[s, 0] * weights[s, :length]
            rest[-1] = 0.0
        else:
            vector = edge[s - 2][-1, own] / unit
            scalars[s, 1] = vector[-1] / weights[s, -1]
            scalars[s, 3] = vector[0] - scalars[s, 1] * weights[s, length]
            rest = vector - scalars[s, 1] * weights[s, length:]
            rest[0] = 0.0
        assert np.abs(rest).max() < 1e-12
        if s > 0:
            scalars[s, 4] = edge[s][0, own[0]]
            scalars[s, 5] = edge[s][0, own[1]] - NEAR
        else:
            scalars[s, 6] = 1.0
            vector = -(1.0 - PIVOT) * derivative[0, rows[1]]
            scalars[s, 7] = vector[-1] / weights[1, -1]
            scalars[s, 8] = vector[0] - scalars[s, 7] * weights[1, length]
        if s + 1 < pieces:
            scalars[s, 9] = edge[s][-1, own[-1]]
            scalars[s, 10] = edge[s][-1, own[-2]] + NEAR
        scalars[s, 11] = unit if s >= 2 else 0.0
        scalars[s, 12] = unit if s < 2 else 0.0
        last = PIVOT - ALPHA * ALPHA / PIVOT if s + 1 < pieces else PIVOT
        scalars[s, 13] = (1.0 - PIVOT / last) / MULT
    return np.concatenate([weights, scalars], axis=1).astype(np.float32)


def lane_order():
    table = np.zeros((256, 256), np.float32)
    for pair in range(2):
        for x in range(64):
            table[128 * pair + 2 * x, 64 * pair + x] = 1.0
            table[128 * pair + (2 * x - 1) % 128, 128 + 64 * pair + x] = 1.0
    return table.astype(jnp.bfloat16)


def end_table(nz):
    table = np.zeros((256, nz), np.float32)
    for half, sign in ((0, 1.0), (128, -1.0)):
        table[half : half + 128 : 2, 0] = sign
        table[half + 1 : half + 128 : 2, nz - 1] = sign
    return table.astype(jnp.bfloat16)


def dot(a, b):
    return jnp.dot(a, b, preferred_element_type=F32)


def dot_nt(a, b):
    return lax.dot_general(a, b, (((1,), (1,)), ((), ())), preferred_element_type=F32)


def iota(shape, axis):
    return lax.broadcasted_iota(jnp.int32, shape, axis)


def split_two(value):
    high = value.astype(BF16)
    return high, (value - high.astype(F32)).astype(BF16)


def gather_kernel(
    fields, table, links, order, f_ref, send, right, left, far, face_y, face_z, keep_y, keep_z
):
    step = pl.program_id(0)
    place = lax.axis_index("ax")
    nx, ny, nz = f_ref.shape[2:]
    lane = iota((ny, nz), 1)

    def group(g, carry):
        to_right, to_left, columns = carry
        part = jnp.zeros((ny, nz), F32)
        for j in range(8):
            x = 8 * g + j
            tile = f_ref[0, 0, x].astype(F32)
            to_right = to_right + table[place, x] * tile
            to_left = to_left + table[place, nx + x] * tile
            turned = pltpu.roll(tile, 2 * j, 1) if j else tile
            part = jnp.where(((lane + 1 - 2 * j) & 127) < 2, turned, part)
        part = pltpu.roll(part, 16 * g, 1)
        columns = jnp.where(((lane + 1 - 16 * g) & 127) < 16, part, columns)
        return to_right, to_left, columns

    zero = jnp.zeros((ny, nz), F32)
    to_right, to_left, columns = lax.fori_loop(0, nx // 8, group, (zero, zero, zero))
    first = f_ref[0, 0, 0]
    last = f_ref[0, 0, nx - 1]
    right[0, 0] = last
    right[0, 1], right[0, 2] = split_two(to_right)
    left[0, 0] = first
    left[0, 1], left[0, 2] = split_two(to_left)
    base = 2 * nx
    far[0] = (
        table[place, base] * to_right
        + table[place, base + 1] * to_left
        + table[place, base + 2] * last.astype(F32)
        + table[place, base + 3] * first.astype(F32)
    ).astype(BF16)
    columns = columns.astype(BF16)
    face_z[0] = columns
    keep_z[step] = columns
    pick = iota((nx, 16 * nx), 1) - 16 * iota((nx, 16 * nx), 0)
    low = dot((pick == 0).astype(F32).astype(BF16), f_ref[0, 0, :, 0:16, :].reshape(16 * nx, nz))
    high = dot(
        (pick == 15).astype(F32).astype(BF16), f_ref[0, 0, :, ny - 16 : ny, :].reshape(16 * nx, nz)
    )
    faces = jnp.concatenate([low, high], axis=1).astype(BF16)
    face_y[0] = faces
    keep_y[step] = faces

    @pl.when(step == fields - 1)
    def _():
        own = lax.axis_index("blk")
        source = links[0]
        blocks, patches = source.shape
        hit = (source == own).astype(F32)
        before = (iota((patches, patches), 0) < iota((patches, patches), 1)).astype(F32)
        rank = dot(hit.astype(BF16), before.astype(BF16))
        face = links[1].astype(F32) + 1.0
        columns = []
        for c in range(2):
            chosen = jnp.where(rank == float(c), hit, 0.0) * face
            chosen = jnp.sum(chosen, axis=1, keepdims=True)
            columns.append(jnp.broadcast_to(chosen, (blocks, 128)))
        chosen = jnp.concatenate(columns, axis=0).astype(BF16)
        rows = 16 * blocks
        row = iota((rows, 2 * blocks), 0)
        slot = (row & 15) // 8 * blocks + row // 16
        spread = (slot == iota((rows, 2 * blocks), 1)).astype(F32).astype(BF16)
        chosen = dot(spread, chosen)
        cells = PW * patches
        target = (chosen.astype(jnp.int32) - 1) * PW + (iota((rows, 128), 0) & 7)
        target = jnp.concatenate([target] * (cells // 128), axis=1)
        chooser = (iota((rows, cells), 1) == target).astype(F32).astype(BF16)
        for pair in range((fields + 1) // 2):
            one = 2 * pair
            if one + 1 < fields:
                ys = jnp.concatenate([keep_y[one], keep_y[one + 1]], axis=0)
                zs = jnp.concatenate([keep_z[one], keep_z[one + 1]], axis=1)
            else:
                ys = jnp.concatenate([keep_y[one], jnp.zeros_like(keep_y[one])], axis=0)
                zs = jnp.concatenate([keep_z[one], jnp.zeros_like(keep_z[one])], axis=1)
            zs = dot(zs, order[...]).astype(BF16)
            zs = jnp.concatenate([zs[:, :128], zs[:, 128:]], axis=0)
            out = dot_nt(chooser[:, : 2 * nz], ys) + dot(chooser[:, 2 * nz :], zs)
            send[:, :, 128 * pair : 128 * pair + 128] = out.astype(BF16).reshape(blocks, 16, 128)


def flux(gradients, metric, density, velocity, pressure, sums):
    ka, kb, kc = metric
    speed = ka * velocity[0] + kb * velocity[1] + kc * velocity[2]
    coupled = density * gradients[0] + pressure * gradients[4]
    turned = ka * gradients[1] + kb * gradients[2] + kc * gradients[3]
    terms = [
        speed * gradients[0],
        speed * gradients[1] + ka * coupled,
        speed * gradients[2] + kb * coupled,
        speed * gradients[3] + kc * coupled,
        speed * gradients[4],
        turned,
    ]
    return terms if sums is None else [a + b for a, b in zip(sums, terms)]


def penalty_parts(fields, nx, links, order, received, face_y, face_z, pen_y, pair_z):
    ny, nz = face_z.shape[1:]
    own = lax.axis_index("blk")
    blocks, patches = links.shape[1:]
    cells = PW * patches
    source = links[0, pl.ds(own, 1), :]
    turn = links[2, pl.ds(own, 1), :]
    same = (patches, patches)
    diagonal = iota(same, 0) == iota(same, 1)

    def tall(value):
        value = jnp.where(diagonal, jnp.broadcast_to(value, same), 0.0)
        return jnp.sum(value, axis=1, keepdims=True)

    wide = jnp.broadcast_to(source, same).astype(F32)
    earlier = (iota(same, 0) < iota(same, 1)) & (wide == tall(source.astype(F32)))
    slot = jnp.sum(earlier.astype(F32), axis=0, keepdims=True)
    live = (source >= 0).astype(F32)
    where = jnp.where(source >= 0, source.astype(F32) * 16.0 + slot * 8.0, -16.0)
    shape = (cells, patches)
    mine = (iota(shape, 0) // PW) == iota(shape, 1)

    def spread(value):
        value = jnp.where(mine, jnp.broadcast_to(value, shape), 0.0)
        return jnp.sum(value, axis=1, keepdims=True)

    cell = iota((cells, 1), 0) & 7
    cell = jnp.where(spread(turn.astype(F32)) > 0.5, 7 - cell, cell)
    target = spread(where).astype(jnp.int32) + cell
    slots = 16 * blocks
    chooser = (iota((cells, slots), 1) == target).astype(F32).astype(BF16)
    live_rows = spread(live)
    got = dot(chooser, received[...].reshape(slots, received.shape[2]))
    got_y = jnp.transpose(got[: 2 * nz])
    shape = (patches, 2 * nz)
    across = jnp.where(
        iota(shape, 0) == iota(shape, 1) // PW, jnp.broadcast_to(tall(live), shape), 0.0
    )
    across = jnp.sum(across, axis=0, keepdims=True)
    for f in range(fields):
        value = got_y[nx * f : nx * f + nx] - across * face_y[f].astype(F32)
        pen_y[0, nx * f : nx * f + nx, :] = value[:, :nz]
        pen_y[1, nx * f : nx * f + nx, :] = value[:, nz:]
    even = (iota((ny, 128), 1) & 1) == 0
    live_z = jnp.where(
        even, live_rows[2 * nz : 2 * nz + ny], live_rows[2 * nz + ny : 2 * nz + 2 * ny]
    )
    for pair in range((fields + 1) // 2):
        lanes = slice(128 * pair, 128 * pair + 128)
        both = jnp.concatenate(
            [got[2 * nz : 2 * nz + ny, lanes], got[2 * nz + ny :, lanes]], axis=1
        )
        both = dot_nt(both.astype(BF16), order[...])
        for q in range(2):
            f = 2 * pair + q
            if f < fields:
                pair_z[f, :, :128] = both[:, 128 * q : 128 * q + 128].astype(BF16)
                pair_z[f, :, 128:] = (live_z * face_z[f].astype(F32)).astype(BF16)


def main_kernel(
    fields,
    table,
    links,
    order,
    along_y,
    along_z,
    ends,
    received,
    right,
    left,
    far,
    own_left,
    face_y,
    face_z,
    adjoint_hbm,
    density_hbm,
    velocity_hbm,
    pressure_hbm,
    metrics_hbm,
    out_hbm,
    f_ref,
    density,
    velocity,
    pressure,
    metrics,
    out,
    line,
    pen_y,
    pair_z,
    field_sem,
    flow_sem,
    out_sem,
):
    place = lax.axis_index("ax")
    nx, ny, nz = density.shape
    rows = 16
    bands = ny // rows
    chunk = 8
    chunks = nx // chunk

    def field_copy(c):
        at = pl.ds(pl.multiple_of(c * rows, rows), rows)
        return pltpu.make_async_copy(
            adjoint_hbm.at[:, 0, :, at, :], f_ref.at[:, :, at, :], field_sem.at[c]
        )

    def flow_copies(c):
        at = pl.ds(c * chunk, chunk)
        return [
            pltpu.make_async_copy(density_hbm.at[0, at], density.at[at], flow_sem.at[c, 0]),
            pltpu.make_async_copy(velocity_hbm.at[:, 0, at], velocity.at[:, at], flow_sem.at[c, 1]),
            pltpu.make_async_copy(pressure_hbm.at[0, at], pressure.at[at], flow_sem.at[c, 2]),
            pltpu.make_async_copy(metrics_hbm.at[:, 0, at], metrics.at[:, at], flow_sem.at[c, 3]),
        ]

    def out_copy(c):
        at = pl.ds(c * chunk, chunk)
        return pltpu.make_async_copy(out.at[:, at], out_hbm.at[:, 0, at], out_sem.at[c])

    for c in range(bands):
        field_copy(c).start()
    for c in reversed(range(chunks)):
        for copy in flow_copies(c):
            copy.start()

    penalty_parts(fields, nx, links, order, received, face_y, face_z, pen_y, pair_z)

    base = 2 * nx

    def scalar(i):
        return table[place, base + i]

    inverse = 1.0 / PIVOT
    near = NEAR * inverse
    far_coef = FAR * inverse

    def band(c, _):
        field_copy(c).wait()
        at = pl.ds(pl.multiple_of(c * rows, rows), rows)

        def load(f, x):
            return f_ref[f, x, at, :].astype(F32)

        def edges(f):
            right_fn = right[f, 1, at, :].astype(F32) + right[f, 2, at, :].astype(F32)
            left_fn = left[f, 1, at, :].astype(F32) + left[f, 2, at, :].astype(F32)
            own_fn = own_left[f, 1, at, :].astype(F32) + own_left[f, 2, at, :].astype(F32)
            right_last = right[f, 0, at, :].astype(F32)
            left_first = left[f, 0, at, :].astype(F32)
            far_plane = far[f, at, :].astype(F32)
            low = (
                right_fn
                + scalar(4) * load(f, 0)
                + scalar(5) * load(f, 1)
                + scalar(6) * own_fn
                + scalar(7) * left_fn
                + scalar(8) * left_first
                + scalar(11) * far_plane
            )
            high = (
                left_fn
                + scalar(9) * load(f, nx - 1)
                + scalar(10) * load(f, nx - 2)
                + scalar(12) * far_plane
            )
            return (
                low * inverse,
                -far_coef * right_last,
                far_coef * left_first,
                high * inverse,
            )

        for members in ((0, 1, 2), (3, 4)):
            edge = [edges(f) for f in members]
            state = []
            for q, f in enumerate(members):
                f0, f1, f2, f3 = [load(f, x) for x in range(4)]
                d0 = near * f1 + far_coef * f2 + edge[q][0]
                d1 = near * (f2 - f0) + far_coef * f3 + edge[q][1] - MULT * d0
                line[f, 0, at, :] = d0
                line[f, 1, at, :] = d1
                state.append((f0, f1, f2, f3, d1))

            def forward(x, state):
                new = []
                for q, f in enumerate(members):
                    fm2, fm1, f0, fp1, d = state[q]
                    fp2 = load(f, x + 2)
                    d = (near * (fp1 - fm1) + far_coef * (fp2 - fm2)) - MULT * d
                    line[f, x, at, :] = d
                    new.append((fm1, f0, fp1, fp2, d))
                return tuple(new)

            state = lax.fori_loop(2, nx - 2, forward, tuple(state), unroll=4)
            for q, f in enumerate(members):
                fm2, fm1, f0, fp1, d = state[q]
                d = near * (fp1 - fm1) - far_coef * fm2 + edge[q][2] - MULT * d
                line[f, nx - 2, at, :] = d
                d = -near * f0 - far_coef * fm1 + edge[q][3] - MULT * d
                line[f, nx - 1, at, :] = d
                line[f, nx, at, :] = scalar(13) * d
        return 0

    lax.fori_loop(0, bands, band, 0)

    lane = iota((ny, 2 * 128), 1)
    row = iota((rows, nz), 0)

    def two(h, _):
        grads_y = []
        grads_z = []
        pens = []
        xs = (2 * h, 2 * h + 1)
        for f in range(fields):
            tiles = [f_ref[f, x] for x in xs]
            both = jnp.concatenate(tiles, axis=0)
            grads_z.append(dot(jnp.concatenate([both, both], axis=1), along_z[...]))
            wide = jnp.concatenate(tiles, axis=1)
            grads_y.append(dot(along_y[...], jnp.concatenate([wide, wide], axis=0)))
            values = pair_z[f]
            chosen = [
                jnp.where(((lane + 1 - 2 * x) & 127) < 2, values, jnp.zeros_like(values)) for x in xs
            ]
            pens.append(dot(jnp.concatenate(chosen, axis=0), ends[...]))
        for q in (1, 0):
            x = xs[q]
            for y in range(0, ny, rows):
                at = slice(y, y + rows)
                rho = density[x, at, :].astype(F32)
                vel = [velocity[i, x, at, :].astype(F32) for i in range(3)]
                press = HEAT * pressure[x, at, :].astype(F32)
                gx = []
                for f in range(fields):
                    value = line[f, x, at, :] - MULT * line[f, x + 1, at, :]
                    line[f, x, at, :] = value
                    gx.append(value)
                gy = [g[at, q * nz : (q + 1) * nz] for g in grads_y]
                gz = [g[q * ny + y : q * ny + y + rows] for g in grads_z]
                sums = None
                for d, g in enumerate((gx, gy, gz)):
                    metric = [metrics[3 * d + i, x, at, :].astype(F32) for i in range(3)]
                    sums = flux(g, metric, rho, vel, press, sums)
                sums[4] = sums[4] + sums[5] / rho
                for f in range(fields):
                    total = sums[f] + pens[f][q * ny + y : q * ny + y + rows]
                    if y == 0:
                        line_y = pen_y[0, pl.ds(f * nx + x, 1), :]
                        total = total + jnp.where(row == 0, line_y, 0.0)
                    if y == ny - rows:
                        line_y = pen_y[1, pl.ds(f * nx + x, 1), :]
                        total = total + jnp.where(row == rows - 1, line_y, 0.0)
                    out[f, x, at, :] = total.astype(BF16)
        return 0

    def section(k, _):
        c = chunks - 1 - k
        for copy in flow_copies(c):
            copy.wait()
        lax.fori_loop(0, chunk // 2, lambda i, s: two(c * (chunk // 2) + chunk // 2 - 1 - i, s), 0)
        out_copy(c).start()
        return 0

    lax.fori_loop(0, chunks, section, 0)
    for c in range(chunks):
        out_copy(c).wait()


def in_hbm(*arrays):
    return [pltpu.with_memory_space_constraint(a, pltpu.HBM) for a in arrays]


def whole(shape):
    return pl.BlockSpec(shape, lambda *_: (0,) * len(shape))


def gather_call(table, order, links, adjoint):
    fields, _, nx, ny, nz = adjoint.shape
    blocks = links.shape[1]
    lanes = 128 * ((fields + 1) // 2)
    shape = jax.ShapeDtypeStruct
    return pl.pallas_call(
        functools.partial(gather_kernel, fields),
        grid=(fields,),
        in_specs=[
            pl.BlockSpec(memory_space=pltpu.SMEM),
            whole(links.shape),
            whole(order.shape),
            pl.BlockSpec((1, 1, nx, ny, nz), lambda i: (i, 0, 0, 0, 0)),
        ],
        out_specs=[
            whole((blocks, 16, lanes)),
            pl.BlockSpec((1, 3, ny, nz), lambda i: (i, 0, 0, 0)),
            pl.BlockSpec((1, 3, ny, nz), lambda i: (i, 0, 0, 0)),
            pl.BlockSpec((1, ny, nz), lambda i: (i, 0, 0)),
            pl.BlockSpec((1, nx, 2 * nz), lambda i: (i, 0, 0)),
            pl.BlockSpec((1, ny, 128), lambda i: (i, 0, 0)),
        ],
        out_shape=[
            shape((blocks, 16, lanes), BF16),
            shape((fields, 3, ny, nz), BF16),
            shape((fields, 3, ny, nz), BF16),
            shape((fields, ny, nz), BF16),
            shape((fields, nx, 2 * nz), BF16),
            shape((fields, ny, 128), BF16),
        ],
        scratch_shapes=[
            pltpu.VMEM((fields, nx, 2 * nz), BF16),
            pltpu.VMEM((fields, ny, 128), BF16),
        ],
        compiler_params=pltpu.CompilerParams(vmem_limit_bytes=16 * MIB),
        cost_estimate=pl.CostEstimate(flops=10**9, bytes_accessed=7 * 10**6, transcendentals=0),
    )(*in_hbm(table, links, order, adjoint))


def main_call(table, order, along_y, along_z, ends, links, flow, edges):
    adjoint = flow[0]
    fields, _, nx, ny, nz = adjoint.shape
    vmem = pl.BlockSpec(memory_space=pltpu.VMEM)
    hbm = pl.BlockSpec(memory_space=pltpu.HBM)
    small = [links, order, along_y, along_z, ends, *edges]
    return pl.pallas_call(
        functools.partial(main_kernel, fields),
        in_specs=[pl.BlockSpec(memory_space=pltpu.SMEM)] + [vmem] * len(small) + [hbm] * len(flow),
        out_specs=hbm,
        out_shape=jax.ShapeDtypeStruct(adjoint.shape, BF16),
        scratch_shapes=[
            pltpu.VMEM((fields, nx, ny, nz), BF16),
            pltpu.VMEM((nx, ny, nz), BF16),
            pltpu.VMEM((3, nx, ny, nz), BF16),
            pltpu.VMEM((nx, ny, nz), BF16),
            pltpu.VMEM((9, nx, ny, nz), BF16),
            pltpu.VMEM((fields, nx, ny, nz), BF16),
            pltpu.VMEM((fields, nx + 1, ny, nz), F32),
            pltpu.VMEM((2, fields * nx, nz), F32),
            pltpu.VMEM((fields, ny, 256), BF16),
            pltpu.SemaphoreType.DMA((ny // 16,)),
            pltpu.SemaphoreType.DMA((nx // 8, 4)),
            pltpu.SemaphoreType.DMA((nx // 8,)),
        ],
        compiler_params=pltpu.CompilerParams(vmem_limit_bytes=52 * MIB),
        cost_estimate=pl.CostEstimate(
            flops=10**10, bytes_accessed=26 * 10**6, transcendentals=0
        ),
    )(*in_hbm(table), *small, *in_hbm(*flow))


def body(tables, adjoint, density, velocity, pressure, metrics, links):
    along_y, along_z, table, order, ends = [jnp.asarray(t) for t in tables]
    send, right, left, far, face_y, face_z = gather_call(table, order, links, adjoint)
    received = lax.all_to_all(send, "blk", 0, 0)
    pieces = lax.axis_size("ax")
    from_left = lax.ppermute(right, "ax", [(i, i + 1) for i in range(pieces - 1)])
    from_right = lax.ppermute(left, "ax", [(i + 1, i) for i in range(pieces - 1)])
    from_far = lax.ppermute(far, "ax", [(i, (i + 2) % pieces) for i in range(pieces)])
    flow = (adjoint, density, velocity, pressure, metrics)
    edges = (received, from_left, from_right, from_far, left, face_y, face_z)
    return main_call(table, order, along_y, along_z, ends, links, flow, edges)


def solution(mesh):
    in_specs = (
        P(None, "blk", "ax", None, None),
        P("blk", "ax", None, None),
        P(None, "blk", "ax", None, None),
        P("blk", "ax", None, None),
        P(None, "blk", "ax", None, None),
        P(),
    )
    out_specs = P(None, "blk", "ax", None, None)

    def run(*args):
        pieces = mesh.shape["ax"]
        nx, ny, nz = args[0].shape[2:]
        tables = (*lateral_tables(ny, nz), axial_tables(pieces, nx // pieces), lane_order())
        tables = (*tables, end_table(nz))
        return jax.shard_map(
            functools.partial(body, tables),
            mesh=mesh,
            in_specs=in_specs,
            out_specs=out_specs,
            check_vma=False,
        )(*args)

    return run
```

```python
import functools

import jax
import jax.numpy as jnp
import numpy as np
from jax import lax
from jax.experimental import pallas as pl
from jax.experimental.pallas import tpu as pltpu
from jax.sharding import PartitionSpec as P

PW = 8
ALPHA = 1.0 / 3.0
NEAR = 7.0 / 9.0
FAR = 1.0 / 36.0
HEAT = 1.4
PIVOT = (1.0 + np.sqrt(1.0 - 4.0 * ALPHA * ALPHA)) / 2.0
MULT = ALPHA / PIVOT
F32 = jnp.float32
BF16 = jnp.bfloat16
MIB = 1 << 20
BATCH = 32


def dense(n):
    eye = functools.partial(np.eye, n)
    left = eye() + ALPHA * (eye(k=1) + eye(k=-1))
    right = NEAR * (eye(k=1) - eye(k=-1)) + FAR * (eye(k=2) - eye(k=-2))
    return left, right


def split(table):
    high = table.astype(np.float32).astype(jnp.bfloat16)
    low = (table - high.astype(np.float64)).astype(jnp.bfloat16)
    return high, low


def lateral_tables(ny, nz):
    left, right = dense(ny)
    high, low = split(np.linalg.solve(left, right))
    along_y = np.concatenate([high, low], axis=1)
    left, right = dense(nz)
    high, low = split(np.linalg.solve(left, right).T)
    along_z = np.concatenate([high, low], axis=0)
    return along_y, along_z


def axial_tables(pieces, length):
    n = pieces * length
    left, right = dense(n)
    derivative = np.linalg.solve(left, right)
    rows = [np.arange(s * length, (s + 1) * length) for s in range(pieces)]
    edge = []
    for s in range(pieces):
        shifted = right[rows[s]].copy()
        for other in (np.arange(0, s * length), np.arange((s + 1) * length, n)):
            if other.size:
                gain = left[np.ix_(rows[s], other)] @ np.linalg.inv(left[np.ix_(other, other)])
                shifted -= gain @ right[other]
        edge.append(shifted)
    weights = np.zeros((pieces, 2 * length))
    scalars = np.zeros((pieces, 16))
    for s in range(pieces):
        own = rows[s]
        if s + 1 < pieces:
            weights[s, :length] = edge[s + 1][0, own]
        if s > 0:
            weights[s, length:] = edge[s - 1][-1, own]
        else:
            weights[s, length:] = -(1.0 - PIVOT) * derivative[0, own]
    unit = abs(edge[2][0, rows[0][-1]])
    for s in range(pieces):
        own = rows[s]
        if s + 2 < pieces:
            vector = edge[s + 2][0, own] / unit
            scalars[s, 0] = vector[0] / weights[s, 0]
            scalars[s, 2] = vector[-1] - scalars[s, 0] * weights[s, length - 1]
            rest = vector - scalars[s, 0] * weights[s, :length]
            rest[-1] = 0.0
        else:
            vector = edge[s - 2][-1, own] / unit
            scalars[s, 1] = vector[-1] / weights[s, -1]
            scalars[s, 3] = vector[0] - scalars[s, 1] * weights[s, length]
            rest = vector - scalars[s, 1] * weights[s, length:]
            rest[0] = 0.0
        assert np.abs(rest).max() < 1e-12
        if s > 0:
            scalars[s, 4] = edge[s][0, own[0]]
            scalars[s, 5] = edge[s][0, own[1]] - NEAR
        else:
            scalars[s, 6] = 1.0
            vector = -(1.0 - PIVOT) * derivative[0, rows[1]]
            scalars[s, 7] = vector[-1] / weights[1, -1]
            scalars[s, 8] = vector[0] - scalars[s, 7] * weights[1, length]
        if s + 1 < pieces:
            scalars[s, 9] = edge[s][-1, own[-1]]
            scalars[s, 10] = edge[s][-1, own[-2]] + NEAR
        scalars[s, 11] = unit if s >= 2 else 0.0
        scalars[s, 12] = unit if s < 2 else 0.0
        last = PIVOT - ALPHA * ALPHA / PIVOT if s + 1 < pieces else PIVOT
        scalars[s, 13] = (1.0 - PIVOT / last) / MULT
    return np.concatenate([weights, scalars], axis=1).astype(np.float32)


def lane_order():
    table = np.zeros((256, 256), np.float32)
    for pair in range(2):
        for x in range(64):
            table[128 * pair + 2 * x, 64 * pair + x] = 1.0
            table[128 * pair + (2 * x - 1) % 128, 128 + 64 * pair + x] = 1.0
    return table.astype(jnp.bfloat16)


def end_table(nz):
    table = np.zeros((256, nz), np.float32)
    for half, sign in ((0, 1.0), (128, -1.0)):
        table[half : half + 128 : 2, 0] = sign
        table[half + 1 : half + 128 : 2, nz - 1] = sign
    return table.astype(jnp.bfloat16)


def dot(a, b):
    return jnp.dot(a, b, preferred_element_type=F32)


def dot_nt(a, b):
    return lax.dot_general(a, b, (((1,), (1,)), ((), ())), preferred_element_type=F32)


def iota(shape, axis):
    return lax.broadcasted_iota(jnp.int32, shape, axis)


def split_two(value):
    high = value.astype(BF16)
    return high, (value - high.astype(F32)).astype(BF16)


def gather_kernel(
    fields,
    table,
    links,
    order,
    adjoint_hbm,
    send,
    right,
    left,
    far,
    face_y,
    face_z,
    f_ref,
    rows_y,
    chooser,
    field_sem,
):
    place = lax.axis_index("ax")
    nx, ny, nz = f_ref.shape[1:]

    def field_copy(f):
        return pltpu.make_async_copy(adjoint_hbm.at[f, 0], f_ref.at[f], field_sem.at[f])

    for f in range(fields):
        field_copy(f).start()

    own = lax.axis_index("blk")
    source = links[0]
    blocks, patches = source.shape
    hit = (source == own).astype(F32)
    before = (iota((patches, patches), 0) < iota((patches, patches), 1)).astype(F32)
    rank = dot(hit.astype(BF16), before.astype(BF16))
    face = links[1].astype(F32) + 1.0
    chosen = []
    for c in range(2):
        value = jnp.where(rank == float(c), hit, 0.0) * face
        value = jnp.sum(value, axis=1, keepdims=True)
        chosen.append(jnp.broadcast_to(value, (blocks, 128)))
    chosen = jnp.concatenate(chosen, axis=0).astype(BF16)
    slots = 16 * blocks
    row = iota((slots, 2 * blocks), 0)
    slot = (row & 15) // 8 * blocks + row // 16
    spread = (slot == iota((slots, 2 * blocks), 1)).astype(F32).astype(BF16)
    chosen = dot(spread, chosen)
    cells = PW * patches
    target = (chosen.astype(jnp.int32) - 1) * PW + (iota((slots, 128), 0) & 7)
    target = jnp.concatenate([target] * (cells // 128), axis=1)
    chooser[...] = (iota((slots, cells), 1) == target).astype(F32).astype(BF16)

    base = 2 * nx
    row8 = iota((8, nz), 0)

    def one_field(f, _):
        field_copy(f).wait()

        def group(g, carry):
            to_right, to_left = carry
            low = jnp.zeros((8, nz), F32)
            high = jnp.zeros((8, nz), F32)
            for j in range(8):
                x = 8 * g + j
                tile = f_ref[f, x].astype(F32)
                to_right = to_right + table[place, x] * tile
                to_left = to_left + table[place, nx + x] * tile
                low = jnp.where(row8 == j, tile[0:1], low)
                high = jnp.where(row8 == j, tile[ny - 1 : ny], high)
            at = pl.ds(pl.multiple_of(8 * g, 8), 8)
            rows_y[at, :nz] = low
            rows_y[at, nz:] = high
            return to_right, to_left

        zero = jnp.zeros((ny, nz), F32)
        to_right, to_left = lax.fori_loop(0, nx // 8, group, (zero, zero))
        first = f_ref[f, 0]
        last = f_ref[f, nx - 1]
        right[f, 0] = last
        right[f, 1], right[f, 2] = split_two(to_right)
        left[f, 0] = first
        left[f, 1], left[f, 2] = split_two(to_left)
        far[f] = (
            table[place, base] * to_right
            + table[place, base + 1] * to_left
            + table[place, base + 2] * last.astype(F32)
            + table[place, base + 3] * first.astype(F32)
        ).astype(BF16)
        face_y[f] = rows_y[...].astype(BF16)
        return 0

    lax.fori_loop(0, fields, one_field, 0)

    row16 = iota((16, 128), 0)
    lane = iota((16, 128), 1)

    def one_hot(mask):
        return mask.astype(F32).astype(BF16)

    def columns(h, total):
        wide = []
        table_rows = []
        for j in range(BATCH):
            x = BATCH * h + j
            wide.append(jnp.concatenate([f_ref[f, x] for f in range(fields)], axis=0))
            table_rows.append(one_hot((row16 == 0) & (lane == 2 * x)))
            table_rows.append(jnp.zeros((nz - 32, 128), BF16))
            table_rows.append(one_hot((row16 == 15) & (lane == ((2 * x - 1) & 127))))
        return total + dot(jnp.concatenate(wide, axis=1), jnp.concatenate(table_rows, axis=0))

    total = lax.fori_loop(0, nx // BATCH, columns, jnp.zeros((fields * ny, 128), F32))
    for f in range(fields):
        face_z[f] = total[f * ny : f * ny + ny].astype(BF16)

    for pair in range((fields + 1) // 2):
        one = 2 * pair
        if one + 1 < fields:
            ys = jnp.concatenate([face_y[one], face_y[one + 1]], axis=0)
            zs = jnp.concatenate([face_z[one], face_z[one + 1]], axis=1)
        else:
            ys = jnp.concatenate([face_y[one], jnp.zeros_like(face_y[one])], axis=0)
            zs = jnp.concatenate([face_z[one], jnp.zeros_like(face_z[one])], axis=1)
        zs = dot(zs, order[...]).astype(BF16)
        zs = jnp.concatenate([zs[:, :128], zs[:, 128:]], axis=0)
        value = dot_nt(chooser[:, : 2 * nz], ys) + dot(chooser[:, 2 * nz :], zs)
        send[:, :, 128 * pair : 128 * pair + 128] = value.astype(BF16).reshape(blocks, 16, 128)


def flux(gradients, metric, density, velocity, pressure, sums):
    ka, kb, kc = metric
    speed = ka * velocity[0] + kb * velocity[1] + kc * velocity[2]
    coupled = density * gradients[0] + pressure * gradients[4]
    turned = ka * gradients[1] + kb * gradients[2] + kc * gradients[3]
    terms = [
        speed * gradients[0],
        speed * gradients[1] + ka * coupled,
        speed * gradients[2] + kb * coupled,
        speed * gradients[3] + kc * coupled,
        speed * gradients[4],
        turned,
    ]
    return terms if sums is None else [a + b for a, b in zip(sums, terms)]


def penalty_parts(fields, nx, links, order, received, face_y, face_z, pen_y, pair_z):
    ny, nz = face_z.shape[1:]
    own = lax.axis_index("blk")
    blocks, patches = links.shape[1:]
    cells = PW * patches
    source = links[0, pl.ds(own, 1), :]
    turn = links[2, pl.ds(own, 1), :]
    same = (patches, patches)
    diagonal = iota(same, 0) == iota(same, 1)

    def tall(value):
        value = jnp.where(diagonal, jnp.broadcast_to(value, same), 0.0)
        return jnp.sum(value, axis=1, keepdims=True)

    wide = jnp.broadcast_to(source, same).astype(F32)
    earlier = (iota(same, 0) < iota(same, 1)) & (wide == tall(source.astype(F32)))
    slot = jnp.sum(earlier.astype(F32), axis=0, keepdims=True)
    live = (source >= 0).astype(F32)
    where = jnp.where(source >= 0, source.astype(F32) * 16.0 + slot * 8.0, -16.0)
    shape = (cells, patches)
    mine = (iota(shape, 0) // PW) == iota(shape, 1)

    def spread(value):
        value = jnp.where(mine, jnp.broadcast_to(value, shape), 0.0)
        return jnp.sum(value, axis=1, keepdims=True)

    cell = iota((cells, 1), 0) & 7
    cell = jnp.where(spread(turn.astype(F32)) > 0.5, 7 - cell, cell)
    target = spread(where).astype(jnp.int32) + cell
    slots = 16 * blocks
    chooser = (iota((cells, slots), 1) == target).astype(F32).astype(BF16)
    live_rows = spread(live)
    got = dot(chooser, received[...].reshape(slots, received.shape[2]))
    got_y = jnp.transpose(got[: 2 * nz])
    shape = (patches, 2 * nz)
    across = jnp.where(
        iota(shape, 0) == iota(shape, 1) // PW, jnp.broadcast_to(tall(live), shape), 0.0
    )
    across = jnp.sum(across, axis=0, keepdims=True)
    for f in range(fields):
        value = got_y[nx * f : nx * f + nx] - across * face_y[f].astype(F32)
        pen_y[0, nx * f : nx * f + nx, :] = value[:, :nz]
        pen_y[1, nx * f : nx * f + nx, :] = value[:, nz:]
    even = (iota((ny, 128), 1) & 1) == 0
    live_z = jnp.where(
        even, live_rows[2 * nz : 2 * nz + ny], live_rows[2 * nz + ny : 2 * nz + 2 * ny]
    )
    for pair in range((fields + 1) // 2):
        lanes = slice(128 * pair, 128 * pair + 128)
        both = jnp.concatenate(
            [got[2 * nz : 2 * nz + ny, lanes], got[2 * nz + ny :, lanes]], axis=1
        )
        both = dot_nt(both.astype(BF16), order[...])
        for q in range(2):
            f = 2 * pair + q
            if f < fields:
                pair_z[f, :, :128] = both[:, 128 * q : 128 * q + 128].astype(BF16)
                pair_z[f, :, 128:] = (live_z * face_z[f].astype(F32)).astype(BF16)


def main_kernel(
    fields,
    table,
    links,
    order,
    along_y,
    along_z,
    ends,
    received,
    right,
    left,
    far,
    own_left,
    face_y,
    face_z,
    adjoint_hbm,
    density_hbm,
    velocity_hbm,
    pressure_hbm,
    metrics_hbm,
    out_hbm,
    f_ref,
    density,
    velocity,
    pressure,
    metrics,
    out,
    line,
    pen_y,
    pair_z,
    now_y,
    now_z,
    now_p,
    later_y,
    later_z,
    later_p,
    field_sem,
    flow_sem,
    out_sem,
):
    place = lax.axis_index("ax")
    nx, ny, nz = density.shape
    rows = 16
    bands = ny // rows
    chunk = 8
    chunks = nx // chunk

    def field_copy(c):
        at = pl.ds(pl.multiple_of(c * rows, rows), rows)
        return pltpu.make_async_copy(
            adjoint_hbm.at[:, 0, :, at, :], f_ref.at[:, :, at, :], field_sem.at[c]
        )

    def flow_copies(c):
        at = pl.ds(c * chunk, chunk)
        return [
            pltpu.make_async_copy(density_hbm.at[0, at], density.at[at], flow_sem.at[c, 0]),
            pltpu.make_async_copy(velocity_hbm.at[:, 0, at], velocity.at[:, at], flow_sem.at[c, 1]),
            pltpu.make_async_copy(pressure_hbm.at[0, at], pressure.at[at], flow_sem.at[c, 2]),
            pltpu.make_async_copy(metrics_hbm.at[:, 0, at], metrics.at[:, at], flow_sem.at[c, 3]),
        ]

    def out_copy(c):
        at = pl.ds(c * chunk, chunk)
        return pltpu.make_async_copy(out.at[:, at], out_hbm.at[:, 0, at], out_sem.at[c])

    for c in range(bands):
        field_copy(c).start()
    for c in reversed(range(chunks)):
        for copy in flow_copies(c):
            copy.start()

    penalty_parts(fields, nx, links, order, received, face_y, face_z, pen_y, pair_z)

    base = 2 * nx

    def scalar(i):
        return table[place, base + i]

    inverse = 1.0 / PIVOT
    near = NEAR * inverse
    far_coef = FAR * inverse

    def band(c, _):
        field_copy(c).wait()
        at = pl.ds(pl.multiple_of(c * rows, rows), rows)

        def load(f, x):
            return f_ref[f, x, at, :].astype(F32)

        def edges(f):
            right_fn = right[f, 1, at, :].astype(F32) + right[f, 2, at, :].astype(F32)
            left_fn = left[f, 1, at, :].astype(F32) + left[f, 2, at, :].astype(F32)
            own_fn = own_left[f, 1, at, :].astype(F32) + own_left[f, 2, at, :].astype(F32)
            right_last = right[f, 0, at, :].astype(F32)
            left_first = left[f, 0, at, :].astype(F32)
            far_plane = far[f, at, :].astype(F32)
            low = (
                right_fn
                + scalar(4) * load(f, 0)
                + scalar(5) * load(f, 1)
                + scalar(6) * own_fn
                + scalar(7) * left_fn
                + scalar(8) * left_first
                + scalar(11) * far_plane
            )
            high = (
                left_fn
                + scalar(9) * load(f, nx - 1)
                + scalar(10) * load(f, nx - 2)
                + scalar(12) * far_plane
            )
            return (
                low * inverse,
                -far_coef * right_last,
                far_coef * left_first,
                high * inverse,
            )

        for members in ((0, 1, 2), (3, 4)):
            edge = [edges(f) for f in members]
            state = []
            for q, f in enumerate(members):
                f0, f1, f2, f3 = [load(f, x) for x in range(4)]
                d0 = near * f1 + far_coef * f2 + edge[q][0]
                d1 = near * (f2 - f0) + far_coef * f3 + edge[q][1] - MULT * d0
                line[f, 0, at, :] = d0
                line[f, 1, at, :] = d1
                state.append((f0, f1, f2, f3, d1))

            def forward(x, state):
                new = []
                for q, f in enumerate(members):
                    fm2, fm1, f0, fp1, d = state[q]
                    fp2 = load(f, x + 2)
                    d = (near * (fp1 - fm1) + far_coef * (fp2 - fm2)) - MULT * d
                    line[f, x, at, :] = d
                    new.append((fm1, f0, fp1, fp2, d))
                return tuple(new)

            state = lax.fori_loop(2, nx - 2, forward, tuple(state), unroll=4)
            for q, f in enumerate(members):
                fm2, fm1, f0, fp1, d = state[q]
                d = near * (fp1 - fm1) - far_coef * fm2 + edge[q][2] - MULT * d
                line[f, nx - 2, at, :] = d
                d = -near * f0 - far_coef * fm1 + edge[q][3] - MULT * d
                line[f, nx - 1, at, :] = d
                line[f, nx, at, :] = scalar(13) * d
        return 0

    lax.fori_loop(0, bands, band, 0)

    lane = iota((rows, 256), 1)
    row = iota((rows, nz), 0)

    def matmuls(h, parts):
        grad_y, grad_z, pens = parts
        xs = (2 * h, 2 * h + 1)
        masks = [(((lane + 1 - 2 * x) & 127) < 2).astype(F32).astype(BF16) for x in xs]
        masks = [jnp.concatenate([mask] * (ny // rows), axis=0) for mask in masks]
        for f in range(fields):
            both = f_ref[f, pl.ds(2 * h, 2)].reshape(2 * ny, nz)
            grad_z[f] = dot(jnp.concatenate([both, both], axis=1), along_z[...])
        for f in range(fields):
            chosen = [pair_z[f] * mask for mask in masks]
            pens[f] = dot(jnp.concatenate(chosen, axis=0), ends[...])
        for f in range(fields):
            wide = jnp.concatenate([f_ref[f, x] for x in xs], axis=1)
            got = dot(along_y[...], jnp.concatenate([wide, wide], axis=0))
            grad_y[f, :ny, :] = got[:, :nz]
            grad_y[f, ny:, :] = got[:, nz:]

    def two_cells(h, parts):
        grad_y, grad_z, pens = parts
        for q in (1, 0):
            x = 2 * h + q
            for y in range(0, ny, rows):
                at = slice(y, y + rows)
                here = slice(q * ny + y, q * ny + y + rows)
                rho = density[x, at, :].astype(F32)
                vel = [velocity[i, x, at, :].astype(F32) for i in range(3)]
                press = HEAT * pressure[x, at, :].astype(F32)
                gx = []
                for f in range(fields):
                    value = line[f, x, at, :] - MULT * line[f, x + 1, at, :]
                    line[f, x, at, :] = value
                    gx.append(value)
                gy = [grad_y[f, here, :] for f in range(fields)]
                gz = [grad_z[f, here, :] for f in range(fields)]
                sums = None
                for d, g in enumerate((gx, gy, gz)):
                    metric = [metrics[3 * d + i, x, at, :].astype(F32) for i in range(3)]
                    sums = flux(g, metric, rho, vel, press, sums)
                sums[4] = sums[4] + sums[5] / rho
                for f in range(fields):
                    total = sums[f] + pens[f, here, :]
                    if y == 0:
                        line_y = pen_y[0, pl.ds(f * nx + x, 1), :]
                        total = total + jnp.where(row == 0, line_y, 0.0)
                    if y == ny - rows:
                        line_y = pen_y[1, pl.ds(f * nx + x, 1), :]
                        total = total + jnp.where(row == rows - 1, line_y, 0.0)
                    out[f, x, at, :] = total.astype(BF16)

    now, later = (now_y, now_z, now_p), (later_y, later_z, later_p)
    matmuls(nx // 2 - 1, now)

    def section(k, _):
        c = chunks - 1 - k
        for copy in flow_copies(c):
            copy.wait()

        def four_cells(i, s):
            h = (c + 1) * (chunk // 2) - 1 - 2 * i
            matmuls(h - 1, later)
            two_cells(h, now)
            matmuls(jnp.maximum(h - 2, 0), now)
            two_cells(h - 1, later)
            return s

        lax.fori_loop(0, chunk // 4, four_cells, 0)
        out_copy(c).start()
        return 0

    lax.fori_loop(0, chunks, section, 0)
    for c in range(chunks):
        out_copy(c).wait()


def in_hbm(*arrays):
    return [pltpu.with_memory_space_constraint(a, pltpu.HBM) for a in arrays]


def gather_call(table, order, links, adjoint):
    fields, _, nx, ny, nz = adjoint.shape
    blocks, patches = links.shape[1:]
    lanes = 128 * ((fields + 1) // 2)
    shape = jax.ShapeDtypeStruct
    vmem = pl.BlockSpec(memory_space=pltpu.VMEM)
    return pl.pallas_call(
        functools.partial(gather_kernel, fields),
        in_specs=[
            pl.BlockSpec(memory_space=pltpu.SMEM),
            vmem,
            vmem,
            pl.BlockSpec(memory_space=pltpu.HBM),
        ],
        out_specs=[vmem] * 6,
        out_shape=[
            shape((blocks, 16, lanes), BF16),
            shape((fields, 3, ny, nz), BF16),
            shape((fields, 3, ny, nz), BF16),
            shape((fields, ny, nz), BF16),
            shape((fields, nx, 2 * nz), BF16),
            shape((fields, ny, 128), BF16),
        ],
        scratch_shapes=[
            pltpu.VMEM((fields, nx, ny, nz), BF16),
            pltpu.VMEM((nx, 2 * nz), F32),
            pltpu.VMEM((16 * blocks, PW * patches), BF16),
            pltpu.SemaphoreType.DMA((fields,)),
        ],
        compiler_params=pltpu.CompilerParams(vmem_limit_bytes=24 * MIB),
        cost_estimate=pl.CostEstimate(flops=10**9, bytes_accessed=7 * 10**6, transcendentals=0),
    )(*in_hbm(table), links, order, *in_hbm(adjoint))


def main_call(table, order, along_y, along_z, ends, links, flow, edges):
    adjoint = flow[0]
    fields, _, nx, ny, nz = adjoint.shape
    vmem = pl.BlockSpec(memory_space=pltpu.VMEM)
    hbm = pl.BlockSpec(memory_space=pltpu.HBM)
    small = [links, order, along_y, along_z, ends, *edges]
    return pl.pallas_call(
        functools.partial(main_kernel, fields),
        in_specs=[pl.BlockSpec(memory_space=pltpu.SMEM)] + [vmem] * len(small) + [hbm] * len(flow),
        out_specs=hbm,
        out_shape=jax.ShapeDtypeStruct(adjoint.shape, BF16),
        scratch_shapes=[
            pltpu.VMEM((fields, nx, ny, nz), BF16),
            pltpu.VMEM((nx, ny, nz), BF16),
            pltpu.VMEM((3, nx, ny, nz), BF16),
            pltpu.VMEM((nx, ny, nz), BF16),
            pltpu.VMEM((9, nx, ny, nz), BF16),
            pltpu.VMEM((fields, nx, ny, nz), BF16),
            pltpu.VMEM((fields, nx + 1, ny, nz), F32),
            pltpu.VMEM((2, fields * nx, nz), F32),
            pltpu.VMEM((fields, ny, 256), BF16),
            *[pltpu.VMEM((fields, 2 * ny, nz), F32) for _ in range(6)],
            pltpu.SemaphoreType.DMA((ny // 16,)),
            pltpu.SemaphoreType.DMA((nx // 8, 4)),
            pltpu.SemaphoreType.DMA((nx // 8,)),
        ],
        compiler_params=pltpu.CompilerParams(vmem_limit_bytes=52 * MIB),
        cost_estimate=pl.CostEstimate(
            flops=10**10, bytes_accessed=26 * 10**6, transcendentals=0
        ),
    )(*in_hbm(table), *small, *in_hbm(*flow))


def body(tables, adjoint, density, velocity, pressure, metrics, links):
    along_y, along_z, table, order, ends = [jnp.asarray(t) for t in tables]
    send, right, left, far, face_y, face_z = gather_call(table, order, links, adjoint)
    received = lax.all_to_all(send, "blk", 0, 0)
    pieces = lax.axis_size("ax")
    from_left = lax.ppermute(right, "ax", [(i, i + 1) for i in range(pieces - 1)])
    from_right = lax.ppermute(left, "ax", [(i + 1, i) for i in range(pieces - 1)])
    from_far = lax.ppermute(far, "ax", [(i, (i + 2) % pieces) for i in range(pieces)])
    flow = (adjoint, density, velocity, pressure, metrics)
    edges = (received, from_left, from_right, from_far, left, face_y, face_z)
    return main_call(table, order, along_y, along_z, ends, links, flow, edges)


def solution(mesh):
    in_specs = (
        P(None, "blk", "ax", None, None),
        P("blk", "ax", None, None),
        P(None, "blk", "ax", None, None),
        P("blk", "ax", None, None),
        P(None, "blk", "ax", None, None),
        P(),
    )
    out_specs = P(None, "blk", "ax", None, None)

    def run(*args):
        pieces = mesh.shape["ax"]
        nx, ny, nz = args[0].shape[2:]
        tables = (*lateral_tables(ny, nz), axial_tables(pieces, nx // pieces), lane_order())
        tables = (*tables, end_table(nz))
        return jax.shard_map(
            functools.partial(body, tables),
            mesh=mesh,
            in_specs=in_specs,
            out_specs=out_specs,
            check_vma=False,
        )(*args)

    return run
```

```python
import functools

import jax
import jax.numpy as jnp
import numpy as np
from jax import lax
from jax.experimental import pallas as pl
from jax.experimental.pallas import tpu as pltpu
from jax.sharding import PartitionSpec as P

PW = 8
ALPHA = 1.0 / 3.0
NEAR = 7.0 / 9.0
FAR = 1.0 / 36.0
HEAT = 1.4
PIVOT = (1.0 + np.sqrt(1.0 - 4.0 * ALPHA * ALPHA)) / 2.0
MULT = ALPHA / PIVOT
F32 = jnp.float32
BF16 = jnp.bfloat16
MIB = 1 << 20
BATCH = 32
BLOCK = 16


def dense(n):
    eye = functools.partial(np.eye, n)
    left = eye() + ALPHA * (eye(k=1) + eye(k=-1))
    right = NEAR * (eye(k=1) - eye(k=-1)) + FAR * (eye(k=2) - eye(k=-2))
    return left, right


def split(table):
    high = table.astype(np.float32).astype(jnp.bfloat16)
    low = (table - high.astype(np.float64)).astype(jnp.bfloat16)
    return high, low


def lateral_tables(ny, nz):
    left, right = dense(ny)
    high, low = split(np.linalg.solve(left, right))
    along_y = np.concatenate([high, low], axis=1)
    left, right = dense(nz)
    high, low = split(np.linalg.solve(left, right).T)
    along_z = np.concatenate([high, low], axis=0)
    return along_y, along_z


def axial_tables(pieces, length):
    n = pieces * length
    left, right = dense(n)
    derivative = np.linalg.solve(left, right)
    rows = [np.arange(s * length, (s + 1) * length) for s in range(pieces)]
    edge = []
    for s in range(pieces):
        shifted = right[rows[s]].copy()
        for other in (np.arange(0, s * length), np.arange((s + 1) * length, n)):
            if other.size:
                gain = left[np.ix_(rows[s], other)] @ np.linalg.inv(left[np.ix_(other, other)])
                shifted -= gain @ right[other]
        edge.append(shifted)
    weights = np.zeros((pieces, 2 * length))
    scalars = np.zeros((pieces, 16))
    for s in range(pieces):
        own = rows[s]
        if s + 1 < pieces:
            weights[s, :length] = edge[s + 1][0, own]
        if s > 0:
            weights[s, length:] = edge[s - 1][-1, own]
        else:
            weights[s, length:] = -(1.0 - PIVOT) * derivative[0, own]
    unit = abs(edge[2][0, rows[0][-1]])
    for s in range(pieces):
        own = rows[s]
        if s + 2 < pieces:
            vector = edge[s + 2][0, own] / unit
            scalars[s, 0] = vector[0] / weights[s, 0]
            scalars[s, 2] = vector[-1] - scalars[s, 0] * weights[s, length - 1]
            rest = vector - scalars[s, 0] * weights[s, :length]
            rest[-1] = 0.0
        else:
            vector = edge[s - 2][-1, own] / unit
            scalars[s, 1] = vector[-1] / weights[s, -1]
            scalars[s, 3] = vector[0] - scalars[s, 1] * weights[s, length]
            rest = vector - scalars[s, 1] * weights[s, length:]
            rest[0] = 0.0
        assert np.abs(rest).max() < 1e-12
        if s > 0:
            scalars[s, 4] = edge[s][0, own[0]]
            scalars[s, 5] = edge[s][0, own[1]] - NEAR
        else:
            scalars[s, 6] = 1.0
            vector = -(1.0 - PIVOT) * derivative[0, rows[1]]
            scalars[s, 7] = vector[-1] / weights[1, -1]
            scalars[s, 8] = vector[0] - scalars[s, 7] * weights[1, length]
        if s + 1 < pieces:
            scalars[s, 9] = edge[s][-1, own[-1]]
            scalars[s, 10] = edge[s][-1, own[-2]] + NEAR
        scalars[s, 11] = unit if s >= 2 else 0.0
        scalars[s, 12] = unit if s < 2 else 0.0
        last = PIVOT - ALPHA * ALPHA / PIVOT if s + 1 < pieces else PIVOT
        scalars[s, 13] = (1.0 - PIVOT / last) / MULT
        scalars[s, 14] = 1.0 if s > 0 else 0.0
        scalars[s, 15] = 1.0 if s + 1 < pieces else 0.0
    return np.concatenate([weights, scalars], axis=1).astype(np.float32)


def lane_order():
    table = np.zeros((256, 256), np.float32)
    for pair in range(2):
        for x in range(64):
            table[128 * pair + 2 * x, 64 * pair + x] = 1.0
            table[128 * pair + (2 * x - 1) % 128, 128 + 64 * pair + x] = 1.0
    return table.astype(jnp.bfloat16)


def end_table(nz):
    table = np.zeros((256, 2 * nz), np.float32)
    for half, sign in ((0, 1.0), (128, -1.0)):
        for lane, column in enumerate((0, 2 * nz - 1, nz, nz - 1)):
            table[half + lane : half + 128 : 4, column] = sign
    return table.astype(jnp.bfloat16)


def dot(a, b):
    return jnp.dot(a, b, preferred_element_type=F32)


def dot_nt(a, b):
    return lax.dot_general(a, b, (((1,), (1,)), ((), ())), preferred_element_type=F32)


def iota(shape, axis):
    return lax.broadcasted_iota(jnp.int32, shape, axis)


def split_two(value):
    high = value.astype(BF16)
    return high, (value - high.astype(F32)).astype(BF16)


def gather_kernel(
    fields,
    table,
    links_hbm,
    order_hbm,
    adjoint_hbm,
    send,
    right,
    left,
    far,
    face_y,
    face_z,
    f_ref,
    rows_y,
    chooser,
    links,
    order,
    field_sem,
    small_sem,
):
    place = lax.axis_index("ax")
    nx, ny, nz = f_ref.shape[1:]

    def field_copy(f):
        return pltpu.make_async_copy(adjoint_hbm.at[f, 0], f_ref.at[f], field_sem.at[f])

    links_copy = pltpu.make_async_copy(links_hbm, links, small_sem.at[0])
    order_copy = pltpu.make_async_copy(order_hbm, order, small_sem.at[1])
    links_copy.start()
    for f in range(fields):
        field_copy(f).start()
    order_copy.start()
    links_copy.wait()

    own = lax.axis_index("blk")
    source = links[0]
    blocks, patches = source.shape
    hit = (source == own).astype(F32)
    before = (iota((patches, patches), 0) < iota((patches, patches), 1)).astype(F32)
    rank = dot(hit.astype(BF16), before.astype(BF16))
    face = links[1].astype(F32) + 1.0
    chosen = []
    for c in range(2):
        value = jnp.where(rank == float(c), hit, 0.0) * face
        value = jnp.sum(value, axis=1, keepdims=True)
        chosen.append(jnp.broadcast_to(value, (blocks, 128)))
    chosen = jnp.concatenate(chosen, axis=0).astype(BF16)
    slots = 16 * blocks
    row = iota((slots, 2 * blocks), 0)
    slot = (row & 15) // 8 * blocks + row // 16
    spread = (slot == iota((slots, 2 * blocks), 1)).astype(F32).astype(BF16)
    chosen = dot(spread, chosen)
    cells = PW * patches
    target = (chosen.astype(jnp.int32) - 1) * PW + (iota((slots, 128), 0) & 7)
    target = jnp.concatenate([target] * (cells // 128), axis=1)
    chooser[...] = (iota((slots, cells), 1) == target).astype(F32).astype(BF16)

    base = 2 * nx
    row8 = iota((8, nz), 0)

    def one_field(f, _):
        field_copy(f).wait()

        def group(g, carry):
            to_right, to_left = carry
            low = jnp.zeros((8, nz), F32)
            high = jnp.zeros((8, nz), F32)
            for j in range(8):
                x = 8 * g + j
                tile = f_ref[f, x].astype(F32)
                to_right = to_right + table[place, x] * tile
                to_left = to_left + table[place, nx + x] * tile
                low = jnp.where(row8 == j, tile[0:1], low)
                high = jnp.where(row8 == j, tile[ny - 1 : ny], high)
            at = pl.ds(pl.multiple_of(8 * g, 8), 8)
            rows_y[at, :nz] = low
            rows_y[at, nz:] = high
            return to_right, to_left

        zero = jnp.zeros((ny, nz), F32)
        to_right, to_left = lax.fori_loop(0, nx // 8, group, (zero, zero))
        first = f_ref[f, 0]
        last = f_ref[f, nx - 1]
        right[f, 0] = last
        right[f, 1], right[f, 2] = split_two(to_right)
        left[f, 0] = first
        left[f, 1], left[f, 2] = split_two(to_left)
        far[f] = (
            table[place, base] * to_right
            + table[place, base + 1] * to_left
            + table[place, base + 2] * last.astype(F32)
            + table[place, base + 3] * first.astype(F32)
        ).astype(BF16)
        face_y[f] = rows_y[...].astype(BF16)
        return 0

    lax.fori_loop(0, fields, one_field, 0)

    row16 = iota((16, 128), 0)
    lane = iota((16, 128), 1)

    def one_hot(mask):
        return mask.astype(F32).astype(BF16)

    def columns(h, total):
        wide = []
        table_rows = []
        for j in range(BATCH):
            x = BATCH * h + j
            wide.append(jnp.concatenate([f_ref[f, x] for f in range(fields)], axis=0))
            table_rows.append(one_hot((row16 == 0) & (lane == 2 * x)))
            table_rows.append(jnp.zeros((nz - 32, 128), BF16))
            table_rows.append(one_hot((row16 == 15) & (lane == ((2 * x - 1) & 127))))
        return total + dot(jnp.concatenate(wide, axis=1), jnp.concatenate(table_rows, axis=0))

    total = lax.fori_loop(0, nx // BATCH, columns, jnp.zeros((fields * ny, 128), F32))
    for f in range(fields):
        face_z[f] = total[f * ny : f * ny + ny].astype(BF16)

    order_copy.wait()
    for pair in range((fields + 1) // 2):
        one = 2 * pair
        if one + 1 < fields:
            ys = jnp.concatenate([face_y[one], face_y[one + 1]], axis=0)
            zs = jnp.concatenate([face_z[one], face_z[one + 1]], axis=1)
        else:
            ys = jnp.concatenate([face_y[one], jnp.zeros_like(face_y[one])], axis=0)
            zs = jnp.concatenate([face_z[one], jnp.zeros_like(face_z[one])], axis=1)
        zs = dot(zs, order[...]).astype(BF16)
        zs = jnp.concatenate([zs[:, :128], zs[:, 128:]], axis=0)
        value = dot_nt(chooser[:, : 2 * nz], ys) + dot(chooser[:, 2 * nz :], zs)
        send[:, :, 128 * pair : 128 * pair + 128] = value.astype(BF16).reshape(blocks, 16, 128)


def flux(gradients, metric, density, velocity, pressure, sums):
    ka, kb, kc = metric
    speed = ka * velocity[0] + kb * velocity[1] + kc * velocity[2]
    coupled = density * gradients[0] + pressure * gradients[4]
    turned = ka * gradients[1] + kb * gradients[2] + kc * gradients[3]
    terms = [
        speed * gradients[0],
        speed * gradients[1] + ka * coupled,
        speed * gradients[2] + kb * coupled,
        speed * gradients[3] + kc * coupled,
        speed * gradients[4],
        turned,
    ]
    return terms if sums is None else [a + b for a, b in zip(sums, terms)]


def penalty_parts(fields, nx, links, order, received, face_y, face_z, pen_y, pair_z):
    ny, nz = face_z.shape[1:]
    own = lax.axis_index("blk")
    blocks, patches = links.shape[1:]
    cells = PW * patches
    source = links[0, pl.ds(own, 1), :]
    turn = links[2, pl.ds(own, 1), :]
    same = (patches, patches)
    diagonal = iota(same, 0) == iota(same, 1)

    def tall(value):
        value = jnp.where(diagonal, jnp.broadcast_to(value, same), 0.0)
        return jnp.sum(value, axis=1, keepdims=True)

    wide = jnp.broadcast_to(source, same).astype(F32)
    earlier = (iota(same, 0) < iota(same, 1)) & (wide == tall(source.astype(F32)))
    slot = jnp.sum(earlier.astype(F32), axis=0, keepdims=True)
    live = (source >= 0).astype(F32)
    where = jnp.where(source >= 0, source.astype(F32) * 16.0 + slot * 8.0, -16.0)
    shape = (cells, patches)
    mine = (iota(shape, 0) // PW) == iota(shape, 1)

    def spread(value):
        value = jnp.where(mine, jnp.broadcast_to(value, shape), 0.0)
        return jnp.sum(value, axis=1, keepdims=True)

    cell = iota((cells, 1), 0) & 7
    cell = jnp.where(spread(turn.astype(F32)) > 0.5, 7 - cell, cell)
    target = spread(where).astype(jnp.int32) + cell
    slots = 16 * blocks
    chooser = (iota((cells, slots), 1) == target).astype(F32).astype(BF16)
    live_rows = spread(live)
    got = dot(chooser, received[...].reshape(slots, received.shape[2]))
    got_y = jnp.transpose(got[: 2 * nz])
    shape = (patches, 2 * nz)
    across = jnp.where(
        iota(shape, 0) == iota(shape, 1) // PW, jnp.broadcast_to(tall(live), shape), 0.0
    )
    across = jnp.sum(across, axis=0, keepdims=True)
    for f in range(fields):
        value = got_y[nx * f : nx * f + nx] - across * face_y[f].astype(F32)
        pen_y[0, nx * f : nx * f + nx, :] = value[:, :nz]
        pen_y[1, nx * f : nx * f + nx, :] = value[:, nz:]
    even = (iota((ny, 128), 1) & 1) == 0
    live_z = jnp.where(
        even, live_rows[2 * nz : 2 * nz + ny], live_rows[2 * nz + ny : 2 * nz + 2 * ny]
    )
    for pair in range((fields + 1) // 2):
        lanes = slice(128 * pair, 128 * pair + 128)
        both = jnp.concatenate(
            [got[2 * nz : 2 * nz + ny, lanes], got[2 * nz + ny :, lanes]], axis=1
        )
        both = dot_nt(both.astype(BF16), order[...])
        for q in range(2):
            f = 2 * pair + q
            if f < fields:
                pair_z[f, :, :128] = both[:, 128 * q : 128 * q + 128].astype(BF16)
                pair_z[f, :, 128:] = (live_z * face_z[f].astype(F32)).astype(BF16)


def main_kernel(
    fields,
    table,
    links,
    order,
    along_y,
    along_z,
    ends,
    received,
    right,
    left,
    far,
    own_left,
    face_y,
    face_z,
    adjoint_hbm,
    density_hbm,
    velocity_hbm,
    pressure_hbm,
    metrics_hbm,
    out_hbm,
    f_ref,
    density,
    velocity,
    pressure,
    metrics,
    out,
    line,
    pen_y,
    pair_z,
    now_y,
    now_z,
    now_p,
    later_y,
    later_z,
    later_p,
    field_sem,
    flow_sem,
    out_sem,
):
    place = lax.axis_index("ax")
    nx, ny, nz = density.shape
    rows = 16
    bands = ny // rows
    chunk = 8
    chunks = nx // chunk

    def field_copy(c):
        at = pl.ds(pl.multiple_of(c * rows, rows), rows)
        return pltpu.make_async_copy(
            adjoint_hbm.at[:, 0, :, at, :], f_ref.at[:, :, at, :], field_sem.at[c]
        )

    def flow_copies(c):
        at = pl.ds(c * chunk, chunk)
        return [
            pltpu.make_async_copy(density_hbm.at[0, at], density.at[at], flow_sem.at[c, 0]),
            pltpu.make_async_copy(velocity_hbm.at[:, 0, at], velocity.at[:, at], flow_sem.at[c, 1]),
            pltpu.make_async_copy(pressure_hbm.at[0, at], pressure.at[at], flow_sem.at[c, 2]),
            pltpu.make_async_copy(metrics_hbm.at[:, 0, at], metrics.at[:, at], flow_sem.at[c, 3]),
        ]

    def out_copy(c):
        at = pl.ds(c * chunk, chunk)
        return pltpu.make_async_copy(out.at[:, at], out_hbm.at[:, 0, at], out_sem.at[c])

    for c in range(bands):
        field_copy(c).start()
    for c in reversed(range(chunks)):
        for copy in flow_copies(c):
            copy.start()

    penalty_parts(fields, nx, links, order, received, face_y, face_z, pen_y, pair_z)

    base = 2 * nx

    def scalar(i):
        return table[place, base + i]

    inverse = 1.0 / PIVOT
    near = NEAR * inverse
    far_coef = FAR * inverse

    def band(c, _):
        field_copy(c).wait()
        at = pl.ds(pl.multiple_of(c * rows, rows), rows)

        def load(f, x):
            return f_ref[f, x, at, :].astype(F32)

        def edges(f):
            right_fn = right[f, 1, at, :].astype(F32) + right[f, 2, at, :].astype(F32)
            left_fn = left[f, 1, at, :].astype(F32) + left[f, 2, at, :].astype(F32)
            own_fn = own_left[f, 1, at, :].astype(F32) + own_left[f, 2, at, :].astype(F32)
            right_last = right[f, 0, at, :].astype(F32)
            left_first = left[f, 0, at, :].astype(F32)
            far_plane = far[f, at, :].astype(F32)
            low = (
                scalar(14) * right_fn
                + scalar(4) * load(f, 0)
                + scalar(5) * load(f, 1)
                + scalar(6) * own_fn
                + scalar(7) * left_fn
                + scalar(8) * left_first
                + scalar(11) * far_plane
            )
            high = (
                scalar(15) * left_fn
                + scalar(9) * load(f, nx - 1)
                + scalar(10) * load(f, nx - 2)
                + scalar(12) * far_plane
            )
            return (
                low * inverse,
                (scalar(14) * -far_coef) * right_last,
                (scalar(15) * far_coef) * left_first,
                high * inverse,
            )

        for members in ((0, 1, 2), (3, 4)):
            edge = [edges(f) for f in members]
            state = []
            for q, f in enumerate(members):
                f0, f1, f2, f3 = [load(f, x) for x in range(4)]
                d0 = near * f1 + far_coef * f2 + edge[q][0]
                d1 = near * (f2 - f0) + far_coef * f3 + edge[q][1] - MULT * d0
                line[f, 0, at, :] = d0
                line[f, 1, at, :] = d1
                state.append((f0, f1, f2, f3, d1))

            def forward(x, state):
                new = []
                for q, f in enumerate(members):
                    fm2, fm1, f0, fp1, d = state[q]
                    fp2 = load(f, x + 2)
                    d = (near * (fp1 - fm1) + far_coef * (fp2 - fm2)) - MULT * d
                    line[f, x, at, :] = d
                    new.append((fm1, f0, fp1, fp2, d))
                return tuple(new)

            state = lax.fori_loop(2, nx - 2, forward, tuple(state), unroll=10)
            for q, f in enumerate(members):
                fm2, fm1, f0, fp1, d = state[q]
                d = near * (fp1 - fm1) - far_coef * fm2 + edge[q][2] - MULT * d
                line[f, nx - 2, at, :] = d
                d = -near * f0 - far_coef * fm1 + edge[q][3] - MULT * d
                line[f, nx - 1, at, :] = d
                line[f, nx, at, :] = scalar(13) * d
        return 0

    lax.fori_loop(0, bands, band, 0)

    lane = iota((rows, 256), 1)
    row = iota((BLOCK, nz), 0)

    def matmuls(h, parts):
        grad_y, grad_z, pens = parts
        mask = (((lane + 1 - 4 * h) & 127) < 4).astype(F32).astype(BF16)
        mask = jnp.concatenate([mask] * (ny // rows), axis=0)

        def along_z_of(f):
            both = f_ref[f, pl.ds(2 * h, 2)].reshape(2 * ny, nz)
            grad_z[f] = dot(jnp.concatenate([both, both], axis=1), along_z[...])

        def pens_of(f):
            got = dot(pair_z[f] * mask, ends[...])
            pens[f, :ny, :] = got[:, :nz]
            pens[f, ny:, :] = got[:, nz:]

        def along_y_of(f):
            wide = jnp.concatenate([f_ref[f, 2 * h], f_ref[f, 2 * h + 1]], axis=1)
            got = dot(along_y[...], jnp.concatenate([wide, wide], axis=0))
            grad_y[f, :ny, :] = got[:, :nz]
            grad_y[f, ny:, :] = got[:, nz:]

        kinds = (along_z_of, pens_of, along_y_of)
        return [functools.partial(kind, f) for kind in kinds for f in range(fields)]

    def two_cells(h, parts, tasks):
        grad_y, grad_z, pens = parts
        blocks = 2 * ny // BLOCK
        number = 0
        for q in (1, 0):
            x = 2 * h + q
            for y in range(0, ny, BLOCK):
                number += 1
                for task in tasks[len(tasks) * (number - 1) // blocks : len(tasks) * number // blocks]:
                    task()
                at = slice(y, y + BLOCK)
                here = slice(q * ny + y, q * ny + y + BLOCK)
                rho = density[x, at, :].astype(F32)
                vel = [velocity[i, x, at, :].astype(F32) for i in range(3)]
                press = HEAT * pressure[x, at, :].astype(F32)
                gx = []
                for f in range(fields):
                    value = line[f, x, at, :] - MULT * line[f, x + 1, at, :]
                    line[f, x, at, :] = value
                    gx.append(value)
                gy = [grad_y[f, here, :] for f in range(fields)]
                gz = [grad_z[f, here, :] for f in range(fields)]
                sums = None
                for d, g in enumerate((gx, gy, gz)):
                    metric = [metrics[3 * d + i, x, at, :].astype(F32) for i in range(3)]
                    sums = flux(g, metric, rho, vel, press, sums)
                sums[4] = sums[4] + sums[5] / rho
                for f in range(fields):
                    total = sums[f] + pens[f, here, :]
                    if y == 0:
                        line_y = pen_y[0, pl.ds(f * nx + x, 1), :]
                        total = total + jnp.where(row == 0, line_y, 0.0)
                    if y == ny - BLOCK:
                        line_y = pen_y[1, pl.ds(f * nx + x, 1), :]
                        total = total + jnp.where(row == BLOCK - 1, line_y, 0.0)
                    out[f, x, at, :] = total.astype(BF16)

    now, later = (now_y, now_z, now_p), (later_y, later_z, later_p)
    for task in matmuls(nx // 2 - 1, now):
        task()

    def section(k, _):
        c = chunks - 1 - k
        for copy in flow_copies(c):
            copy.wait()

        def four_cells(i, s):
            h = (c + 1) * (chunk // 2) - 1 - 2 * i
            two_cells(h, now, matmuls(h - 1, later))
            two_cells(h - 1, later, matmuls(jnp.maximum(h - 2, 0), now))
            return s

        lax.fori_loop(0, chunk // 4, four_cells, 0)
        out_copy(c).start()
        return 0

    lax.fori_loop(0, chunks, section, 0)
    for c in range(chunks):
        out_copy(c).wait()


def in_hbm(*arrays):
    return [pltpu.with_memory_space_constraint(a, pltpu.HBM) for a in arrays]


def gather_call(table, order, links, adjoint):
    fields, _, nx, ny, nz = adjoint.shape
    blocks, patches = links.shape[1:]
    lanes = 128 * ((fields + 1) // 2)
    shape = jax.ShapeDtypeStruct
    vmem = pl.BlockSpec(memory_space=pltpu.VMEM)
    return pl.pallas_call(
        functools.partial(gather_kernel, fields),
        in_specs=[pl.BlockSpec(memory_space=pltpu.SMEM)]
        + [pl.BlockSpec(memory_space=pltpu.HBM)] * 3,
        out_specs=[vmem] * 6,
        out_shape=[
            shape((blocks, 16, lanes), BF16),
            shape((fields, 3, ny, nz), BF16),
            shape((fields, 3, ny, nz), BF16),
            shape((fields, ny, nz), BF16),
            shape((fields, nx, 2 * nz), BF16),
            shape((fields, ny, 128), BF16),
        ],
        scratch_shapes=[
            pltpu.VMEM((fields, nx, ny, nz), BF16),
            pltpu.VMEM((nx, 2 * nz), F32),
            pltpu.VMEM((16 * blocks, PW * patches), BF16),
            pltpu.VMEM(links.shape, jnp.int32),
            pltpu.VMEM(order.shape, BF16),
            pltpu.SemaphoreType.DMA((fields,)),
            pltpu.SemaphoreType.DMA((2,)),
        ],
        compiler_params=pltpu.CompilerParams(vmem_limit_bytes=24 * MIB),
        cost_estimate=pl.CostEstimate(flops=10**9, bytes_accessed=7 * 10**6, transcendentals=0),
    )(*in_hbm(table, links, order, adjoint))


def main_call(table, order, along_y, along_z, ends, links, flow, edges):
    adjoint = flow[0]
    fields, _, nx, ny, nz = adjoint.shape
    vmem = pl.BlockSpec(memory_space=pltpu.VMEM)
    hbm = pl.BlockSpec(memory_space=pltpu.HBM)
    small = [links, order, along_y, along_z, ends, *edges]
    return pl.pallas_call(
        functools.partial(main_kernel, fields),
        in_specs=[pl.BlockSpec(memory_space=pltpu.SMEM)] + [vmem] * len(small) + [hbm] * len(flow),
        out_specs=hbm,
        out_shape=jax.ShapeDtypeStruct(adjoint.shape, BF16),
        scratch_shapes=[
            pltpu.VMEM((fields, nx, ny, nz), BF16),
            pltpu.VMEM((nx, ny, nz), BF16),
            pltpu.VMEM((3, nx, ny, nz), BF16),
            pltpu.VMEM((nx, ny, nz), BF16),
            pltpu.VMEM((9, nx, ny, nz), BF16),
            pltpu.VMEM((fields, nx, ny, nz), BF16),
            pltpu.VMEM((fields, nx + 1, ny, nz), F32),
            pltpu.VMEM((2, fields * nx, nz), F32),
            pltpu.VMEM((fields, ny, 256), BF16),
            *[pltpu.VMEM((fields, 2 * ny, nz), F32) for _ in range(6)],
            pltpu.SemaphoreType.DMA((ny // 16,)),
            pltpu.SemaphoreType.DMA((nx // 8, 4)),
            pltpu.SemaphoreType.DMA((nx // 8,)),
        ],
        compiler_params=pltpu.CompilerParams(vmem_limit_bytes=52 * MIB),
        cost_estimate=pl.CostEstimate(
            flops=10**10, bytes_accessed=26 * 10**6, transcendentals=0
        ),
    )(*in_hbm(table), *small, *in_hbm(*flow))


def body(tables, adjoint, density, velocity, pressure, metrics, links):
    along_y, along_z, table, order, ends = [jnp.asarray(t) for t in tables]
    send, right, left, far, face_y, face_z = gather_call(table, order, links, adjoint)
    received = lax.all_to_all(send, "blk", 0, 0)
    pieces = lax.axis_size("ax")
    from_left = lax.ppermute(right, "ax", [(i, (i + 1) % pieces) for i in range(pieces)])
    from_right = lax.ppermute(left, "ax", [((i + 1) % pieces, i) for i in range(pieces)])
    from_far = lax.ppermute(far, "ax", [(i, (i + 2) % pieces) for i in range(pieces)])
    flow = (adjoint, density, velocity, pressure, metrics)
    edges = (received, from_left, from_right, from_far, left, face_y, face_z)
    return main_call(table, order, along_y, along_z, ends, links, flow, edges)


def solution(mesh):
    in_specs = (
        P(None, "blk", "ax", None, None),
        P("blk", "ax", None, None),
        P(None, "blk", "ax", None, None),
        P("blk", "ax", None, None),
        P(None, "blk", "ax", None, None),
        P(),
    )
    out_specs = P(None, "blk", "ax", None, None)

    def run(*args):
        pieces = mesh.shape["ax"]
        nx, ny, nz = args[0].shape[2:]
        tables = (*lateral_tables(ny, nz), axial_tables(pieces, nx // pieces), lane_order())
        tables = (*tables, end_table(nz))
        return jax.shard_map(
            functools.partial(body, tables),
            mesh=mesh,
            in_specs=in_specs,
            out_specs=out_specs,
            check_vma=False,
        )(*args)

    return run
```

```python
import functools

import jax
import jax.numpy as jnp
import numpy as np
from jax import lax
from jax.experimental import pallas as pl
from jax.experimental.pallas import tpu as pltpu
from jax.sharding import PartitionSpec as P

PW = 8
ALPHA = 1.0 / 3.0
NEAR = 7.0 / 9.0
FAR = 1.0 / 36.0
HEAT = 1.4
PIVOT = (1.0 + np.sqrt(1.0 - 4.0 * ALPHA * ALPHA)) / 2.0
MULT = ALPHA / PIVOT
F32 = jnp.float32
BF16 = jnp.bfloat16
MIB = 1 << 20
BATCH = 32
BLOCK = 16
READY = 24
LATERAL_CHUNK = 8


def dense(n):
    eye = functools.partial(np.eye, n)
    left = eye() + ALPHA * (eye(k=1) + eye(k=-1))
    right = NEAR * (eye(k=1) - eye(k=-1)) + FAR * (eye(k=2) - eye(k=-2))
    return left, right


def split(table):
    high = table.astype(np.float32).astype(jnp.bfloat16)
    low = (table - high.astype(np.float64)).astype(jnp.bfloat16)
    return high, low


def lateral_tables(ny, nz):
    left, right = dense(ny)
    high, low = split(np.linalg.solve(left, right))
    along_y = np.concatenate([high, low], axis=1)
    left, right = dense(nz)
    high, low = split(np.linalg.solve(left, right).T)
    along_z = np.concatenate([high, low], axis=0)
    return along_y, along_z


def axial_tables(pieces, length):
    n = pieces * length
    left, right = dense(n)
    derivative = np.linalg.solve(left, right)
    rows = [np.arange(s * length, (s + 1) * length) for s in range(pieces)]
    edge = []
    for s in range(pieces):
        shifted = right[rows[s]].copy()
        for other in (np.arange(0, s * length), np.arange((s + 1) * length, n)):
            if other.size:
                gain = left[np.ix_(rows[s], other)] @ np.linalg.inv(left[np.ix_(other, other)])
                shifted -= gain @ right[other]
        edge.append(shifted)
    weights = np.zeros((pieces, 2 * length))
    scalars = np.zeros((pieces, 16))
    for s in range(pieces):
        own = rows[s]
        if s + 1 < pieces:
            weights[s, :length] = edge[s + 1][0, own]
        if s > 0:
            weights[s, length:] = edge[s - 1][-1, own]
        else:
            weights[s, length:] = -(1.0 - PIVOT) * derivative[0, own]
    unit = abs(edge[2][0, rows[0][-1]])
    for s in range(pieces):
        own = rows[s]
        if s + 2 < pieces:
            vector = edge[s + 2][0, own] / unit
            scalars[s, 0] = vector[0] / weights[s, 0]
            scalars[s, 2] = vector[-1] - scalars[s, 0] * weights[s, length - 1]
            rest = vector - scalars[s, 0] * weights[s, :length]
            rest[-1] = 0.0
        else:
            vector = edge[s - 2][-1, own] / unit
            scalars[s, 1] = vector[-1] / weights[s, -1]
            scalars[s, 3] = vector[0] - scalars[s, 1] * weights[s, length]
            rest = vector - scalars[s, 1] * weights[s, length:]
            rest[0] = 0.0
        assert np.abs(rest).max() < 1e-12
        if s > 0:
            scalars[s, 4] = edge[s][0, own[0]]
            scalars[s, 5] = edge[s][0, own[1]] - NEAR
        else:
            scalars[s, 6] = 1.0
            vector = -(1.0 - PIVOT) * derivative[0, rows[1]]
            scalars[s, 7] = vector[-1] / weights[1, -1]
            scalars[s, 8] = vector[0] - scalars[s, 7] * weights[1, length]
        if s + 1 < pieces:
            scalars[s, 9] = edge[s][-1, own[-1]]
            scalars[s, 10] = edge[s][-1, own[-2]] + NEAR
        scalars[s, 11] = unit if s >= 2 else 0.0
        scalars[s, 12] = unit if s < 2 else 0.0
        last = PIVOT - ALPHA * ALPHA / PIVOT if s + 1 < pieces else PIVOT
        scalars[s, 13] = (1.0 - PIVOT / last) / MULT
        scalars[s, 14] = 1.0 if s > 0 else 0.0
        scalars[s, 15] = 1.0 if s + 1 < pieces else 0.0
    return np.concatenate([weights, scalars], axis=1).astype(np.float32)


def lane_order():
    table = np.zeros((256, 256), np.float32)
    for pair in range(2):
        for x in range(64):
            table[128 * pair + 2 * x, 64 * pair + x] = 1.0
            table[128 * pair + (2 * x - 1) % 128, 128 + 64 * pair + x] = 1.0
    return table.astype(jnp.bfloat16)


def end_table(nz):
    table = np.zeros((256, 2 * nz), np.float32)
    for half, sign in ((0, 1.0), (128, -1.0)):
        for lane, column in enumerate((0, 2 * nz - 1, nz, nz - 1)):
            table[half + lane : half + 128 : 4, column] = sign
    return table.astype(jnp.bfloat16)


def dot(a, b):
    return jnp.dot(a, b, preferred_element_type=F32)


def dot_nt(a, b):
    return lax.dot_general(a, b, (((1,), (1,)), ((), ())), preferred_element_type=F32)


def iota(shape, axis):
    return lax.broadcasted_iota(jnp.int32, shape, axis)


def split_two(value):
    high = value.astype(BF16)
    return high, (value - high.astype(F32)).astype(BF16)


def gather_kernel(
    fields,
    table,
    links_hbm,
    order_hbm,
    adjoint_hbm,
    send,
    right,
    left,
    far,
    face_y,
    face_z,
    f_ref,
    rows_y,
    chooser,
    links,
    order,
    field_sem,
    small_sem,
):
    place = lax.axis_index("ax")
    nx, ny, nz = f_ref.shape[1:]

    def field_copy(f):
        return pltpu.make_async_copy(adjoint_hbm.at[f, 0], f_ref.at[f], field_sem.at[f])

    links_copy = pltpu.make_async_copy(links_hbm, links, small_sem.at[0])
    order_copy = pltpu.make_async_copy(order_hbm, order, small_sem.at[1])
    links_copy.start()
    for f in range(fields):
        field_copy(f).start()
    order_copy.start()
    links_copy.wait()

    own = lax.axis_index("blk")
    source = links[0]
    blocks, patches = source.shape
    hit = (source == own).astype(F32)
    before = (iota((patches, patches), 0) < iota((patches, patches), 1)).astype(F32)
    rank = dot(hit.astype(BF16), before.astype(BF16))
    face = links[1].astype(F32) + 1.0
    chosen = []
    for c in range(2):
        value = jnp.where(rank == float(c), hit, 0.0) * face
        value = jnp.sum(value, axis=1, keepdims=True)
        chosen.append(jnp.broadcast_to(value, (blocks, 128)))
    chosen = jnp.concatenate(chosen, axis=0).astype(BF16)
    slots = 16 * blocks
    row = iota((slots, 2 * blocks), 0)
    slot = (row & 15) // 8 * blocks + row // 16
    spread = (slot == iota((slots, 2 * blocks), 1)).astype(F32).astype(BF16)
    chosen = dot(spread, chosen)
    cells = PW * patches
    target = (chosen.astype(jnp.int32) - 1) * PW + (iota((slots, 128), 0) & 7)
    target = jnp.concatenate([target] * (cells // 128), axis=1)
    chooser[...] = (iota((slots, cells), 1) == target).astype(F32).astype(BF16)

    base = 2 * nx
    row8 = iota((8, nz), 0)

    def one_field(f, _):
        field_copy(f).wait()

        def group(g, carry):
            to_right, to_left = carry
            low = jnp.zeros((8, nz), F32)
            high = jnp.zeros((8, nz), F32)
            for j in range(8):
                x = 8 * g + j
                tile = f_ref[f, x].astype(F32)
                to_right = to_right + table[place, x] * tile
                to_left = to_left + table[place, nx + x] * tile
                low = jnp.where(row8 == j, tile[0:1], low)
                high = jnp.where(row8 == j, tile[ny - 1 : ny], high)
            at = pl.ds(pl.multiple_of(8 * g, 8), 8)
            rows_y[at, :nz] = low
            rows_y[at, nz:] = high
            return to_right, to_left

        zero = jnp.zeros((ny, nz), F32)
        to_right, to_left = lax.fori_loop(0, nx // 8, group, (zero, zero))
        first = f_ref[f, 0]
        last = f_ref[f, nx - 1]
        right[f, 0] = last
        right[f, 1], right[f, 2] = split_two(to_right)
        left[f, 0] = first
        left[f, 1], left[f, 2] = split_two(to_left)
        far[f] = (
            table[place, base] * to_right
            + table[place, base + 1] * to_left
            + table[place, base + 2] * last.astype(F32)
            + table[place, base + 3] * first.astype(F32)
        ).astype(BF16)
        face_y[f] = rows_y[...].astype(BF16)
        return 0

    lax.fori_loop(0, fields, one_field, 0)

    row16 = iota((16, 128), 0)
    lane = iota((16, 128), 1)

    def one_hot(mask):
        return mask.astype(F32).astype(BF16)

    def columns(h, total):
        wide = []
        table_rows = []
        for j in range(BATCH):
            x = BATCH * h + j
            wide.append(jnp.concatenate([f_ref[f, x] for f in range(fields)], axis=0))
            table_rows.append(one_hot((row16 == 0) & (lane == 2 * x)))
            table_rows.append(jnp.zeros((nz - 32, 128), BF16))
            table_rows.append(one_hot((row16 == 15) & (lane == ((2 * x - 1) & 127))))
        return total + dot(jnp.concatenate(wide, axis=1), jnp.concatenate(table_rows, axis=0))

    total = lax.fori_loop(0, nx // BATCH, columns, jnp.zeros((fields * ny, 128), F32))
    for f in range(fields):
        face_z[f] = total[f * ny : f * ny + ny].astype(BF16)

    order_copy.wait()
    for pair in range((fields + 1) // 2):
        one = 2 * pair
        if one + 1 < fields:
            ys = jnp.concatenate([face_y[one], face_y[one + 1]], axis=0)
            zs = jnp.concatenate([face_z[one], face_z[one + 1]], axis=1)
        else:
            ys = jnp.concatenate([face_y[one], jnp.zeros_like(face_y[one])], axis=0)
            zs = jnp.concatenate([face_z[one], jnp.zeros_like(face_z[one])], axis=1)
        zs = dot(zs, order[...]).astype(BF16)
        zs = jnp.concatenate([zs[:, :128], zs[:, 128:]], axis=0)
        value = dot_nt(chooser[:, : 2 * nz], ys) + dot(chooser[:, 2 * nz :], zs)
        send[:, :, 128 * pair : 128 * pair + 128] = value.astype(BF16).reshape(blocks, 16, 128)


def flux(gradients, metric, density, velocity, pressure, sums):
    ka, kb, kc = metric
    speed = ka * velocity[0] + kb * velocity[1] + kc * velocity[2]
    coupled = density * gradients[0] + pressure * gradients[4]
    turned = ka * gradients[1] + kb * gradients[2] + kc * gradients[3]
    terms = [
        speed * gradients[0],
        speed * gradients[1] + ka * coupled,
        speed * gradients[2] + kb * coupled,
        speed * gradients[3] + kc * coupled,
        speed * gradients[4],
        turned,
    ]
    return terms if sums is None else [a + b for a, b in zip(sums, terms)]


def lateral_kernel(fields, along_y, along_z, f_ref, density, velocity, pressure, ky, kz, out):
    chunk, ny, nz = f_ref.shape[2:]

    def body(h, _):
        grads_y = []
        grads_z = []
        xs = (2 * h, 2 * h + 1)
        for f in range(fields):
            tiles = [f_ref[f, 0, x] for x in xs]
            both = jnp.concatenate(tiles, axis=0)
            grads_z.append(dot(jnp.concatenate([both, both], axis=1), along_z[...]))
        for f in range(fields):
            wide = jnp.concatenate([f_ref[f, 0, x] for x in xs], axis=1)
            grads_y.append(dot(along_y[...], jnp.concatenate([wide, wide], axis=0)))
        for q, x in enumerate(xs):
            for y in range(0, ny, 16):
                at = slice(y, y + 16)
                rho = density[0, x, at, :].astype(F32)
                vel = [velocity[i, 0, x, at, :].astype(F32) for i in range(3)]
                press = HEAT * pressure[0, x, at, :].astype(F32)
                gy = [g[at, q * nz : (q + 1) * nz] for g in grads_y]
                gz = [g[q * ny + y : q * ny + y + 16] for g in grads_z]
                sums = None
                for g, k in ((gy, ky), (gz, kz)):
                    metric = [k[i, 0, x, at, :].astype(F32) for i in range(3)]
                    sums = flux(g, metric, rho, vel, press, sums)
                for i in range(4):
                    out[i, x, at, :] = sums[i]
                out[4, x, at, :] = sums[4] + sums[5] / rho
        return 0

    lax.fori_loop(0, chunk // 2, body, 0)


def penalty_parts(fields, nx, links, order, received, face_y, face_z, pen_y, pair_z):
    ny, nz = face_z.shape[1:]
    own = lax.axis_index("blk")
    blocks, patches = links.shape[1:]
    cells = PW * patches
    source = links[0, pl.ds(own, 1), :]
    turn = links[2, pl.ds(own, 1), :]
    same = (patches, patches)
    diagonal = iota(same, 0) == iota(same, 1)

    def tall(value):
        value = jnp.where(diagonal, jnp.broadcast_to(value, same), 0.0)
        return jnp.sum(value, axis=1, keepdims=True)

    wide = jnp.broadcast_to(source, same).astype(F32)
    earlier = (iota(same, 0) < iota(same, 1)) & (wide == tall(source.astype(F32)))
    slot = jnp.sum(earlier.astype(F32), axis=0, keepdims=True)
    live = (source >= 0).astype(F32)
    where = jnp.where(source >= 0, source.astype(F32) * 16.0 + slot * 8.0, -16.0)
    shape = (cells, patches)
    mine = (iota(shape, 0) // PW) == iota(shape, 1)

    def spread(value):
        value = jnp.where(mine, jnp.broadcast_to(value, shape), 0.0)
        return jnp.sum(value, axis=1, keepdims=True)

    cell = iota((cells, 1), 0) & 7
    cell = jnp.where(spread(turn.astype(F32)) > 0.5, 7 - cell, cell)
    target = spread(where).astype(jnp.int32) + cell
    slots = 16 * blocks
    chooser = (iota((cells, slots), 1) == target).astype(F32).astype(BF16)
    live_rows = spread(live)
    got = dot(chooser, received[...].reshape(slots, received.shape[2]))
    got_y = jnp.transpose(got[: 2 * nz])
    shape = (patches, 2 * nz)
    across = jnp.where(
        iota(shape, 0) == iota(shape, 1) // PW, jnp.broadcast_to(tall(live), shape), 0.0
    )
    across = jnp.sum(across, axis=0, keepdims=True)
    for f in range(fields):
        value = got_y[nx * f : nx * f + nx] - across * face_y[f].astype(F32)
        pen_y[0, nx * f : nx * f + nx, :] = value[:, :nz]
        pen_y[1, nx * f : nx * f + nx, :] = value[:, nz:]
    even = (iota((ny, 128), 1) & 1) == 0
    live_z = jnp.where(
        even, live_rows[2 * nz : 2 * nz + ny], live_rows[2 * nz + ny : 2 * nz + 2 * ny]
    )
    for pair in range((fields + 1) // 2):
        lanes = slice(128 * pair, 128 * pair + 128)
        both = jnp.concatenate(
            [got[2 * nz : 2 * nz + ny, lanes], got[2 * nz + ny :, lanes]], axis=1
        )
        both = dot_nt(both.astype(BF16), order[...])
        for q in range(2):
            f = 2 * pair + q
            if f < fields:
                pair_z[f, :, :128] = both[:, 128 * q : 128 * q + 128].astype(BF16)
                pair_z[f, :, 128:] = (live_z * face_z[f].astype(F32)).astype(BF16)


def main_kernel(
    fields,
    table,
    links,
    order,
    along_y,
    along_z,
    ends,
    received,
    right,
    left,
    far,
    own_left,
    face_y,
    face_z,
    adjoint_hbm,
    density_hbm,
    velocity_hbm,
    pressure_hbm,
    metrics_hbm,
    partial_hbm,
    out_hbm,
    f_ref,
    density,
    velocity,
    pressure,
    metrics,
    partial,
    out,
    line,
    pen_y,
    pair_z,
    now_y,
    now_z,
    now_p,
    later_y,
    later_z,
    later_p,
    field_sem,
    flow_sem,
    out_sem,
):
    place = lax.axis_index("ax")
    nx, ny, nz = density.shape
    rows = 16
    bands = ny // rows
    chunk = 8
    chunks = nx // chunk

    def field_copy(c):
        at = pl.ds(pl.multiple_of(c * rows, rows), rows)
        return pltpu.make_async_copy(
            adjoint_hbm.at[:, 0, :, at, :], f_ref.at[:, :, at, :], field_sem.at[c]
        )

    ready = partial.shape[1] // chunk

    def flow_copies(c, done):
        at = pl.ds(c * chunk, chunk)
        some = pl.ds(0, 3 if done else 9)
        copies = [
            pltpu.make_async_copy(density_hbm.at[0, at], density.at[at], flow_sem.at[c, 0]),
            pltpu.make_async_copy(velocity_hbm.at[:, 0, at], velocity.at[:, at], flow_sem.at[c, 1]),
            pltpu.make_async_copy(pressure_hbm.at[0, at], pressure.at[at], flow_sem.at[c, 2]),
            pltpu.make_async_copy(
                metrics_hbm.at[some, 0, at], metrics.at[some, at], flow_sem.at[c, 3]
            ),
        ]
        if done:
            copies.append(
                pltpu.make_async_copy(partial_hbm.at[:, at], partial.at[:, at], flow_sem.at[c, 4])
            )
        return copies

    def out_copy(c):
        at = pl.ds(c * chunk, chunk)
        return pltpu.make_async_copy(out.at[:, at], out_hbm.at[:, 0, at], out_sem.at[c])

    for c in range(bands):
        field_copy(c).start()
    for c in reversed(range(chunks)):
        for copy in flow_copies(c, c < ready):
            copy.start()

    penalty_parts(fields, nx, links, order, received, face_y, face_z, pen_y, pair_z)

    base = 2 * nx

    def scalar(i):
        return table[place, base + i]

    inverse = 1.0 / PIVOT
    near = NEAR * inverse
    far_coef = FAR * inverse

    def band(c, _):
        field_copy(c).wait()
        at = pl.ds(pl.multiple_of(c * rows, rows), rows)

        def load(f, x):
            return f_ref[f, x, at, :].astype(F32)

        def edges(f):
            right_fn = right[f, 1, at, :].astype(F32) + right[f, 2, at, :].astype(F32)
            left_fn = left[f, 1, at, :].astype(F32) + left[f, 2, at, :].astype(F32)
            own_fn = own_left[f, 1, at, :].astype(F32) + own_left[f, 2, at, :].astype(F32)
            right_last = right[f, 0, at, :].astype(F32)
            left_first = left[f, 0, at, :].astype(F32)
            far_plane = far[f, at, :].astype(F32)
            low = (
                scalar(14) * right_fn
                + scalar(4) * load(f, 0)
                + scalar(5) * load(f, 1)
                + scalar(6) * own_fn
                + scalar(7) * left_fn
                + scalar(8) * left_first
                + scalar(11) * far_plane
            )
            high = (
                scalar(15) * left_fn
                + scalar(9) * load(f, nx - 1)
                + scalar(10) * load(f, nx - 2)
                + scalar(12) * far_plane
            )
            return (
                low * inverse,
                (scalar(14) * -far_coef) * right_last,
                (scalar(15) * far_coef) * left_first,
                high * inverse,
            )

        for members in ((0, 1, 2), (3, 4)):
            edge = [edges(f) for f in members]
            state = []
            for q, f in enumerate(members):
                f0, f1, f2, f3 = [load(f, x) for x in range(4)]
                d0 = near * f1 + far_coef * f2 + edge[q][0]
                d1 = near * (f2 - f0) + far_coef * f3 + edge[q][1] - MULT * d0
                line[f, 0, at, :] = d0
                line[f, 1, at, :] = d1
                state.append((f0, f1, f2, f3, d1))

            def forward(x, state):
                new = []
                for q, f in enumerate(members):
                    fm2, fm1, f0, fp1, d = state[q]
                    fp2 = load(f, x + 2)
                    d = (near * (fp1 - fm1) + far_coef * (fp2 - fm2)) - MULT * d
                    line[f, x, at, :] = d
                    new.append((fm1, f0, fp1, fp2, d))
                return tuple(new)

            state = lax.fori_loop(2, nx - 2, forward, tuple(state), unroll=10)
            for q, f in enumerate(members):
                fm2, fm1, f0, fp1, d = state[q]
                d = near * (fp1 - fm1) - far_coef * fm2 + edge[q][2] - MULT * d
                line[f, nx - 2, at, :] = d
                d = -near * f0 - far_coef * fm1 + edge[q][3] - MULT * d
                line[f, nx - 1, at, :] = d
                line[f, nx, at, :] = scalar(13) * d
        return 0

    lax.fori_loop(0, bands, band, 0)

    lane = iota((rows, 256), 1)
    row = iota((BLOCK, nz), 0)

    def matmuls(h, parts, done=False):
        grad_y, grad_z, pens = parts
        mask = (((lane + 1 - 4 * h) & 127) < 4).astype(F32).astype(BF16)
        mask = jnp.concatenate([mask] * (ny // rows), axis=0)

        def along_z_of(f):
            both = f_ref[f, pl.ds(2 * h, 2)].reshape(2 * ny, nz)
            grad_z[f] = dot(jnp.concatenate([both, both], axis=1), along_z[...])

        def pens_of(f):
            got = dot(pair_z[f] * mask, ends[...])
            pens[f, :ny, :] = got[:, :nz]
            pens[f, ny:, :] = got[:, nz:]

        def along_y_of(f):
            wide = jnp.concatenate([f_ref[f, 2 * h], f_ref[f, 2 * h + 1]], axis=1)
            got = dot(along_y[...], jnp.concatenate([wide, wide], axis=0))
            grad_y[f, :ny, :] = got[:, :nz]
            grad_y[f, ny:, :] = got[:, nz:]

        kinds = (pens_of,) if done else (along_z_of, pens_of, along_y_of)
        return [functools.partial(kind, f) for kind in kinds for f in range(fields)]

    def two_cells(h, parts, tasks, done=False):
        grad_y, grad_z, pens = parts
        blocks = 2 * ny // BLOCK
        number = 0
        for q in (1, 0):
            x = 2 * h + q
            for y in range(0, ny, BLOCK):
                number += 1
                for task in tasks[len(tasks) * (number - 1) // blocks : len(tasks) * number // blocks]:
                    task()
                at = slice(y, y + BLOCK)
                here = slice(q * ny + y, q * ny + y + BLOCK)
                rho = density[x, at, :].astype(F32)
                vel = [velocity[i, x, at, :].astype(F32) for i in range(3)]
                press = HEAT * pressure[x, at, :].astype(F32)
                gx = []
                for f in range(fields):
                    value = line[f, x, at, :] - MULT * line[f, x + 1, at, :]
                    line[f, x, at, :] = value
                    gx.append(value)
                grads = [gx]
                if not done:
                    grads.append([grad_y[f, here, :] for f in range(fields)])
                    grads.append([grad_z[f, here, :] for f in range(fields)])
                sums = None
                for d, g in enumerate(grads):
                    metric = [metrics[3 * d + i, x, at, :].astype(F32) for i in range(3)]
                    sums = flux(g, metric, rho, vel, press, sums)
                sums[4] = sums[4] + sums[5] / rho
                for f in range(fields):
                    total = sums[f] + pens[f, here, :]
                    if done:
                        total = total + partial[f, x, at, :]
                    if y == 0:
                        line_y = pen_y[0, pl.ds(f * nx + x, 1), :]
                        total = total + jnp.where(row == 0, line_y, 0.0)
                    if y == ny - BLOCK:
                        line_y = pen_y[1, pl.ds(f * nx + x, 1), :]
                        total = total + jnp.where(row == BLOCK - 1, line_y, 0.0)
                    out[f, x, at, :] = total.astype(BF16)

    now, later = (now_y, now_z, now_p), (later_y, later_z, later_p)
    for task in matmuls(nx // 2 - 1, now):
        task()

    def section(k, _, done=False):
        c = chunks - 1 - k
        for copy in flow_copies(c, done):
            copy.wait()

        def four_cells(i, s):
            h = (c + 1) * (chunk // 2) - 1 - 2 * i
            two_cells(h, now, matmuls(h - 1, later, done), done)
            two_cells(h - 1, later, matmuls(jnp.maximum(h - 2, 0), now, done), done)
            return s

        lax.fori_loop(0, chunk // 4, four_cells, 0)
        out_copy(c).start()
        return 0

    lax.fori_loop(0, chunks - ready, section, 0)
    lax.fori_loop(chunks - ready, chunks, functools.partial(section, done=True), 0)
    for c in range(chunks):
        out_copy(c).wait()


def in_hbm(*arrays):
    return [pltpu.with_memory_space_constraint(a, pltpu.HBM) for a in arrays]


def gather_call(table, order, links, adjoint):
    fields, _, nx, ny, nz = adjoint.shape
    blocks, patches = links.shape[1:]
    lanes = 128 * ((fields + 1) // 2)
    shape = jax.ShapeDtypeStruct
    vmem = pl.BlockSpec(memory_space=pltpu.VMEM)
    return pl.pallas_call(
        functools.partial(gather_kernel, fields),
        in_specs=[pl.BlockSpec(memory_space=pltpu.SMEM)]
        + [pl.BlockSpec(memory_space=pltpu.HBM)] * 3,
        out_specs=[vmem] * 6,
        out_shape=[
            shape((blocks, 16, lanes), BF16),
            shape((fields, 3, ny, nz), BF16),
            shape((fields, 3, ny, nz), BF16),
            shape((fields, ny, nz), BF16),
            shape((fields, nx, 2 * nz), BF16),
            shape((fields, ny, 128), BF16),
        ],
        scratch_shapes=[
            pltpu.VMEM((fields, nx, ny, nz), BF16),
            pltpu.VMEM((nx, 2 * nz), F32),
            pltpu.VMEM((16 * blocks, PW * patches), BF16),
            pltpu.VMEM(links.shape, jnp.int32),
            pltpu.VMEM(order.shape, BF16),
            pltpu.SemaphoreType.DMA((fields,)),
            pltpu.SemaphoreType.DMA((2,)),
        ],
        compiler_params=pltpu.CompilerParams(vmem_limit_bytes=24 * MIB),
        cost_estimate=pl.CostEstimate(flops=10**9, bytes_accessed=7 * 10**6, transcendentals=0),
    )(*in_hbm(table, links, order, adjoint))


def lateral_call(along_y, along_z, adjoint, density, velocity, pressure, metrics):
    fields, _, nx, ny, nz = adjoint.shape
    chunk = LATERAL_CHUNK
    fixed = (lambda i: (0, 0))
    return pl.pallas_call(
        functools.partial(lateral_kernel, fields),
        grid=(READY // chunk,),
        in_specs=[
            pl.BlockSpec(along_y.shape, fixed),
            pl.BlockSpec(along_z.shape, fixed),
            pl.BlockSpec((fields, 1, chunk, ny, nz), lambda i: (0, 0, i, 0, 0)),
            pl.BlockSpec((1, chunk, ny, nz), lambda i: (0, i, 0, 0)),
            pl.BlockSpec((3, 1, chunk, ny, nz), lambda i: (0, 0, i, 0, 0)),
            pl.BlockSpec((1, chunk, ny, nz), lambda i: (0, i, 0, 0)),
            pl.BlockSpec((3, 1, chunk, ny, nz), lambda i: (1, 0, i, 0, 0)),
            pl.BlockSpec((3, 1, chunk, ny, nz), lambda i: (2, 0, i, 0, 0)),
        ],
        out_specs=pl.BlockSpec((fields, chunk, ny, nz), lambda i: (0, i, 0, 0)),
        out_shape=pltpu.HBM((fields, READY, ny, nz), F32),
        compiler_params=pltpu.CompilerParams(vmem_limit_bytes=24 * MIB),
        cost_estimate=pl.CostEstimate(
            flops=10**10, bytes_accessed=27 * 10**6, transcendentals=0
        ),
    )(*in_hbm(along_y, along_z, adjoint, density, velocity, pressure, metrics, metrics))


def main_call(table, order, along_y, along_z, ends, links, flow, partial, edges):
    adjoint = flow[0]
    fields, _, nx, ny, nz = adjoint.shape
    vmem = pl.BlockSpec(memory_space=pltpu.VMEM)
    hbm = pl.BlockSpec(memory_space=pltpu.HBM)
    small = [links, order, along_y, along_z, ends, *edges]
    return pl.pallas_call(
        functools.partial(main_kernel, fields),
        in_specs=[pl.BlockSpec(memory_space=pltpu.SMEM)]
        + [vmem] * len(small)
        + [hbm] * (len(flow) + 1),
        out_specs=hbm,
        out_shape=jax.ShapeDtypeStruct(adjoint.shape, BF16),
        scratch_shapes=[
            pltpu.VMEM((fields, nx, ny, nz), BF16),
            pltpu.VMEM((nx, ny, nz), BF16),
            pltpu.VMEM((3, nx, ny, nz), BF16),
            pltpu.VMEM((nx, ny, nz), BF16),
            pltpu.VMEM((9, nx, ny, nz), BF16),
            pltpu.VMEM(partial.shape, F32),
            pltpu.VMEM((fields, nx, ny, nz), BF16),
            pltpu.VMEM((fields, nx + 1, ny, nz), F32),
            pltpu.VMEM((2, fields * nx, nz), F32),
            pltpu.VMEM((fields, ny, 256), BF16),
            *[pltpu.VMEM((fields, 2 * ny, nz), F32) for _ in range(6)],
            pltpu.SemaphoreType.DMA((ny // 16,)),
            pltpu.SemaphoreType.DMA((nx // 8, 5)),
            pltpu.SemaphoreType.DMA((nx // 8,)),
        ],
        compiler_params=pltpu.CompilerParams(vmem_limit_bytes=52 * MIB),
        cost_estimate=pl.CostEstimate(
            flops=10**10, bytes_accessed=26 * 10**6, transcendentals=0
        ),
    )(*in_hbm(table), *small, *in_hbm(*flow, partial))


def body(tables, adjoint, density, velocity, pressure, metrics, links):
    along_y, along_z, table, order, ends = [jnp.asarray(t) for t in tables]
    send, right, left, far, face_y, face_z = gather_call(table, order, links, adjoint)
    received = lax.all_to_all(send, "blk", 0, 0)
    pieces = lax.axis_size("ax")
    from_left = lax.ppermute(right, "ax", [(i, (i + 1) % pieces) for i in range(pieces)])
    from_right = lax.ppermute(left, "ax", [((i + 1) % pieces, i) for i in range(pieces)])
    from_far = lax.ppermute(far, "ax", [(i, (i + 2) % pieces) for i in range(pieces)])
    flow = (adjoint, density, velocity, pressure, metrics)
    partial = lateral_call(along_y, along_z, *flow)
    edges = (received, from_left, from_right, from_far, left, face_y, face_z)
    return main_call(table, order, along_y, along_z, ends, links, flow, partial, edges)


def solution(mesh):
    in_specs = (
        P(None, "blk", "ax", None, None),
        P("blk", "ax", None, None),
        P(None, "blk", "ax", None, None),
        P("blk", "ax", None, None),
        P(None, "blk", "ax", None, None),
        P(),
    )
    out_specs = P(None, "blk", "ax", None, None)

    def run(*args):
        pieces = mesh.shape["ax"]
        nx, ny, nz = args[0].shape[2:]
        tables = (*lateral_tables(ny, nz), axial_tables(pieces, nx // pieces), lane_order())
        tables = (*tables, end_table(nz))
        return jax.shard_map(
            functools.partial(body, tables),
            mesh=mesh,
            in_specs=in_specs,
            out_specs=out_specs,
            check_vma=False,
        )(*args)

    return run
```

```python
import functools

import jax
import jax.numpy as jnp
import numpy as np
from jax import lax
from jax.experimental import pallas as pl
from jax.experimental.pallas import tpu as pltpu
from jax.sharding import PartitionSpec as P

PW = 8
ALPHA = 1.0 / 3.0
NEAR = 7.0 / 9.0
FAR = 1.0 / 36.0
HEAT = 1.4
PIVOT = (1.0 + np.sqrt(1.0 - 4.0 * ALPHA * ALPHA)) / 2.0
MULT = ALPHA / PIVOT
F32 = jnp.float32
BF16 = jnp.bfloat16
MIB = 1 << 20
BATCH = 32
BLOCK = 16
READY = 24
LATERAL_CHUNK = 12


def dense(n):
    eye = functools.partial(np.eye, n)
    left = eye() + ALPHA * (eye(k=1) + eye(k=-1))
    right = NEAR * (eye(k=1) - eye(k=-1)) + FAR * (eye(k=2) - eye(k=-2))
    return left, right


def split(table):
    high = table.astype(np.float32).astype(jnp.bfloat16)
    low = (table - high.astype(np.float64)).astype(jnp.bfloat16)
    return high, low


def lateral_tables(ny, nz):
    left, right = dense(ny)
    high, low = split(np.linalg.solve(left, right))
    along_y = np.concatenate([high, low], axis=1)
    left, right = dense(nz)
    high, low = split(np.linalg.solve(left, right).T)
    along_z = np.concatenate([high, low], axis=0)
    return along_y, along_z


def axial_tables(pieces, length):
    n = pieces * length
    left, right = dense(n)
    derivative = np.linalg.solve(left, right)
    rows = [np.arange(s * length, (s + 1) * length) for s in range(pieces)]
    edge = []
    for s in range(pieces):
        shifted = right[rows[s]].copy()
        for other in (np.arange(0, s * length), np.arange((s + 1) * length, n)):
            if other.size:
                gain = left[np.ix_(rows[s], other)] @ np.linalg.inv(left[np.ix_(other, other)])
                shifted -= gain @ right[other]
        edge.append(shifted)
    weights = np.zeros((pieces, 2 * length))
    scalars = np.zeros((pieces, 16))
    for s in range(pieces):
        own = rows[s]
        if s + 1 < pieces:
            weights[s, :length] = edge[s + 1][0, own]
        if s > 0:
            weights[s, length:] = edge[s - 1][-1, own]
        else:
            weights[s, length:] = -(1.0 - PIVOT) * derivative[0, own]
    unit = abs(edge[2][0, rows[0][-1]])
    for s in range(pieces):
        own = rows[s]
        if s + 2 < pieces:
            vector = edge[s + 2][0, own] / unit
            scalars[s, 0] = vector[0] / weights[s, 0]
            scalars[s, 2] = vector[-1] - scalars[s, 0] * weights[s, length - 1]
            rest = vector - scalars[s, 0] * weights[s, :length]
            rest[-1] = 0.0
        else:
            vector = edge[s - 2][-1, own] / unit
            scalars[s, 1] = vector[-1] / weights[s, -1]
            scalars[s, 3] = vector[0] - scalars[s, 1] * weights[s, length]
            rest = vector - scalars[s, 1] * weights[s, length:]
            rest[0] = 0.0
        assert np.abs(rest).max() < 1e-12
        if s > 0:
            scalars[s, 4] = edge[s][0, own[0]]
            scalars[s, 5] = edge[s][0, own[1]] - NEAR
        else:
            scalars[s, 6] = 1.0
            vector = -(1.0 - PIVOT) * derivative[0, rows[1]]
            scalars[s, 7] = vector[-1] / weights[1, -1]
            scalars[s, 8] = vector[0] - scalars[s, 7] * weights[1, length]
        if s + 1 < pieces:
            scalars[s, 9] = edge[s][-1, own[-1]]
            scalars[s, 10] = edge[s][-1, own[-2]] + NEAR
        scalars[s, 11] = unit if s >= 2 else 0.0
        scalars[s, 12] = unit if s < 2 else 0.0
        last = PIVOT - ALPHA * ALPHA / PIVOT if s + 1 < pieces else PIVOT
        scalars[s, 13] = (1.0 - PIVOT / last) / MULT
        scalars[s, 14] = 1.0 if s > 0 else 0.0
        scalars[s, 15] = 1.0 if s + 1 < pieces else 0.0
    return np.concatenate([weights, scalars], axis=1).astype(np.float32)


def lane_order():
    table = np.zeros((256, 256), np.float32)
    for pair in range(2):
        for x in range(64):
            table[128 * pair + 2 * x, 64 * pair + x] = 1.0
            table[128 * pair + (2 * x - 1) % 128, 128 + 64 * pair + x] = 1.0
    return table.astype(jnp.bfloat16)


def end_table(nz):
    table = np.zeros((256, 2 * nz), np.float32)
    for half, sign in ((0, 1.0), (128, -1.0)):
        for lane, column in enumerate((0, 2 * nz - 1, nz, nz - 1)):
            table[half + lane : half + 128 : 4, column] = sign
    return table.astype(jnp.bfloat16)


def dot(a, b):
    return jnp.dot(a, b, preferred_element_type=F32)


def dot_nt(a, b):
    return lax.dot_general(a, b, (((1,), (1,)), ((), ())), preferred_element_type=F32)


def iota(shape, axis):
    return lax.broadcasted_iota(jnp.int32, shape, axis)


def split_two(value):
    high = value.astype(BF16)
    return high, (value - high.astype(F32)).astype(BF16)


def gather_kernel(
    fields,
    table,
    links_hbm,
    order_hbm,
    adjoint_hbm,
    send,
    right,
    left,
    far,
    face_y,
    face_z,
    f_ref,
    rows_y,
    chooser,
    links,
    order,
    field_sem,
    small_sem,
):
    place = lax.axis_index("ax")
    nx, ny, nz = f_ref.shape[1:]

    def field_copy(f):
        return pltpu.make_async_copy(adjoint_hbm.at[f, 0], f_ref.at[f], field_sem.at[f])

    links_copy = pltpu.make_async_copy(links_hbm, links, small_sem.at[0])
    order_copy = pltpu.make_async_copy(order_hbm, order, small_sem.at[1])
    links_copy.start()
    for f in range(fields):
        field_copy(f).start()
    order_copy.start()
    links_copy.wait()

    own = lax.axis_index("blk")
    source = links[0]
    blocks, patches = source.shape
    hit = (source == own).astype(F32)
    before = (iota((patches, patches), 0) < iota((patches, patches), 1)).astype(F32)
    rank = dot(hit.astype(BF16), before.astype(BF16))
    face = links[1].astype(F32) + 1.0
    chosen = []
    for c in range(2):
        value = jnp.where(rank == float(c), hit, 0.0) * face
        value = jnp.sum(value, axis=1, keepdims=True)
        chosen.append(jnp.broadcast_to(value, (blocks, 128)))
    chosen = jnp.concatenate(chosen, axis=0).astype(BF16)
    slots = 16 * blocks
    row = iota((slots, 2 * blocks), 0)
    slot = (row & 15) // 8 * blocks + row // 16
    spread = (slot == iota((slots, 2 * blocks), 1)).astype(F32).astype(BF16)
    chosen = dot(spread, chosen)
    cells = PW * patches
    target = (chosen.astype(jnp.int32) - 1) * PW + (iota((slots, 128), 0) & 7)
    target = jnp.concatenate([target] * (cells // 128), axis=1)
    chooser[...] = (iota((slots, cells), 1) == target).astype(F32).astype(BF16)

    base = 2 * nx
    row8 = iota((8, nz), 0)

    def one_field(f, _):
        field_copy(f).wait()

        def group(g, carry):
            to_right, to_left = carry
            low = jnp.zeros((8, nz), F32)
            high = jnp.zeros((8, nz), F32)
            for j in range(8):
                x = 8 * g + j
                tile = f_ref[f, x].astype(F32)
                to_right = to_right + table[place, x] * tile
                to_left = to_left + table[place, nx + x] * tile
                low = jnp.where(row8 == j, tile[0:1], low)
                high = jnp.where(row8 == j, tile[ny - 1 : ny], high)
            at = pl.ds(pl.multiple_of(8 * g, 8), 8)
            rows_y[at, :nz] = low
            rows_y[at, nz:] = high
            return to_right, to_left

        zero = jnp.zeros((ny, nz), F32)
        to_right, to_left = lax.fori_loop(0, nx // 8, group, (zero, zero), unroll=2)
        first = f_ref[f, 0]
        last = f_ref[f, nx - 1]
        right[f, 0] = last
        right[f, 1], right[f, 2] = split_two(to_right)
        left[f, 0] = first
        left[f, 1], left[f, 2] = split_two(to_left)
        far[f] = (
            table[place, base] * to_right
            + table[place, base + 1] * to_left
            + table[place, base + 2] * last.astype(F32)
            + table[place, base + 3] * first.astype(F32)
        ).astype(BF16)
        face_y[f] = rows_y[...].astype(BF16)
        return 0

    lax.fori_loop(0, fields, one_field, 0)

    row16 = iota((16, 128), 0)
    lane = iota((16, 128), 1)

    def one_hot(mask):
        return mask.astype(F32).astype(BF16)

    def columns(h, total):
        wide = []
        table_rows = []
        for j in range(BATCH):
            x = BATCH * h + j
            wide.append(jnp.concatenate([f_ref[f, x] for f in range(fields)], axis=0))
            table_rows.append(one_hot((row16 == 0) & (lane == 2 * x)))
            table_rows.append(jnp.zeros((nz - 32, 128), BF16))
            table_rows.append(one_hot((row16 == 15) & (lane == ((2 * x - 1) & 127))))
        return total + dot(jnp.concatenate(wide, axis=1), jnp.concatenate(table_rows, axis=0))

    total = lax.fori_loop(0, nx // BATCH, columns, jnp.zeros((fields * ny, 128), F32))
    for f in range(fields):
        face_z[f] = total[f * ny : f * ny + ny].astype(BF16)

    order_copy.wait()
    for pair in range((fields + 1) // 2):
        one = 2 * pair
        if one + 1 < fields:
            ys = jnp.concatenate([face_y[one], face_y[one + 1]], axis=0)
            zs = jnp.concatenate([face_z[one], face_z[one + 1]], axis=1)
        else:
            ys = jnp.concatenate([face_y[one], jnp.zeros_like(face_y[one])], axis=0)
            zs = jnp.concatenate([face_z[one], jnp.zeros_like(face_z[one])], axis=1)
        zs = dot(zs, order[...]).astype(BF16)
        zs = jnp.concatenate([zs[:, :128], zs[:, 128:]], axis=0)
        value = dot_nt(chooser[:, : 2 * nz], ys) + dot(chooser[:, 2 * nz :], zs)
        send[:, :, 128 * pair : 128 * pair + 128] = value.astype(BF16).reshape(blocks, 16, 128)


def flux(gradients, metric, density, velocity, pressure, sums):
    ka, kb, kc = metric
    speed = ka * velocity[0] + kb * velocity[1] + kc * velocity[2]
    coupled = density * gradients[0] + pressure * gradients[4]
    turned = ka * gradients[1] + kb * gradients[2] + kc * gradients[3]
    terms = [
        speed * gradients[0],
        speed * gradients[1] + ka * coupled,
        speed * gradients[2] + kb * coupled,
        speed * gradients[3] + kc * coupled,
        speed * gradients[4],
        turned,
    ]
    return terms if sums is None else [a + b for a, b in zip(sums, terms)]


def lateral_kernel(fields, along_y, along_z, f_ref, density, velocity, pressure, ky, kz, out):
    chunk, ny, nz = f_ref.shape[2:]

    def body(h, _):
        grads_y = []
        grads_z = []
        xs = (2 * h, 2 * h + 1)
        for f in range(fields):
            tiles = [f_ref[f, 0, x] for x in xs]
            both = jnp.concatenate(tiles, axis=0)
            grads_z.append(dot(jnp.concatenate([both, both], axis=1), along_z[...]))
        for f in range(fields):
            wide = jnp.concatenate([f_ref[f, 0, x] for x in xs], axis=1)
            grads_y.append(dot(along_y[...], jnp.concatenate([wide, wide], axis=0)))
        for q, x in enumerate(xs):
            for y in range(0, ny, 16):
                at = slice(y, y + 16)
                rho = density[0, x, at, :].astype(F32)
                vel = [velocity[i, 0, x, at, :].astype(F32) for i in range(3)]
                press = HEAT * pressure[0, x, at, :].astype(F32)
                gy = [g[at, q * nz : (q + 1) * nz] for g in grads_y]
                gz = [g[q * ny + y : q * ny + y + 16] for g in grads_z]
                sums = None
                for g, k in ((gy, ky), (gz, kz)):
                    metric = [k[i, 0, x, at, :].astype(F32) for i in range(3)]
                    sums = flux(g, metric, rho, vel, press, sums)
                for i in range(4):
                    out[i, x, at, :] = sums[i]
                out[4, x, at, :] = sums[4] + sums[5] / rho
        return 0

    lax.fori_loop(0, chunk // 2, body, 0)


def penalty_parts(fields, nx, links, order, received, face_y, face_z, pen_y, pair_z):
    ny, nz = face_z.shape[1:]
    own = lax.axis_index("blk")
    blocks, patches = links.shape[1:]
    cells = PW * patches
    source = links[0, pl.ds(own, 1), :]
    turn = links[2, pl.ds(own, 1), :]
    same = (patches, patches)
    diagonal = iota(same, 0) == iota(same, 1)

    def tall(value):
        value = jnp.where(diagonal, jnp.broadcast_to(value, same), 0.0)
        return jnp.sum(value, axis=1, keepdims=True)

    wide = jnp.broadcast_to(source, same).astype(F32)
    earlier = (iota(same, 0) < iota(same, 1)) & (wide == tall(source.astype(F32)))
    slot = jnp.sum(earlier.astype(F32), axis=0, keepdims=True)
    live = (source >= 0).astype(F32)
    where = jnp.where(source >= 0, source.astype(F32) * 16.0 + slot * 8.0, -16.0)
    shape = (cells, patches)
    mine = (iota(shape, 0) // PW) == iota(shape, 1)

    def spread(value):
        value = jnp.where(mine, jnp.broadcast_to(value, shape), 0.0)
        return jnp.sum(value, axis=1, keepdims=True)

    cell = iota((cells, 1), 0) & 7
    cell = jnp.where(spread(turn.astype(F32)) > 0.5, 7 - cell, cell)
    target = spread(where).astype(jnp.int32) + cell
    slots = 16 * blocks
    chooser = (iota((cells, slots), 1) == target).astype(F32).astype(BF16)
    live_rows = spread(live)
    got = dot(chooser, received[...].reshape(slots, received.shape[2]))
    got_y = jnp.transpose(got[: 2 * nz])
    shape = (patches, 2 * nz)
    across = jnp.where(
        iota(shape, 0) == iota(shape, 1) // PW, jnp.broadcast_to(tall(live), shape), 0.0
    )
    across = jnp.sum(across, axis=0, keepdims=True)
    for f in range(fields):
        value = got_y[nx * f : nx * f + nx] - across * face_y[f].astype(F32)
        pen_y[0, nx * f : nx * f + nx, :] = value[:, :nz]
        pen_y[1, nx * f : nx * f + nx, :] = value[:, nz:]
    even = (iota((ny, 128), 1) & 1) == 0
    live_z = jnp.where(
        even, live_rows[2 * nz : 2 * nz + ny], live_rows[2 * nz + ny : 2 * nz + 2 * ny]
    )
    for pair in range((fields + 1) // 2):
        lanes = slice(128 * pair, 128 * pair + 128)
        both = jnp.concatenate(
            [got[2 * nz : 2 * nz + ny, lanes], got[2 * nz + ny :, lanes]], axis=1
        )
        both = dot_nt(both.astype(BF16), order[...])
        for q in range(2):
            f = 2 * pair + q
            if f < fields:
                pair_z[f, :, :128] = both[:, 128 * q : 128 * q + 128].astype(BF16)
                pair_z[f, :, 128:] = (live_z * face_z[f].astype(F32)).astype(BF16)


def main_kernel(
    fields,
    table,
    links,
    order,
    along_y,
    along_z,
    ends,
    received,
    right,
    left,
    far,
    own_left,
    face_y,
    face_z,
    adjoint_hbm,
    density_hbm,
    velocity_hbm,
    pressure_hbm,
    metrics_hbm,
    partial_hbm,
    out_hbm,
    f_ref,
    density,
    velocity,
    pressure,
    metrics,
    partial,
    out,
    line,
    pen_y,
    pair_z,
    now_y,
    now_z,
    now_p,
    later_y,
    later_z,
    later_p,
    field_sem,
    flow_sem,
    out_sem,
):
    place = lax.axis_index("ax")
    nx, ny, nz = density.shape
    rows = 16
    bands = ny // rows
    chunk = 8
    chunks = nx // chunk

    def field_copy(c):
        at = pl.ds(pl.multiple_of(c * rows, rows), rows)
        return pltpu.make_async_copy(
            adjoint_hbm.at[:, 0, :, at, :], f_ref.at[:, :, at, :], field_sem.at[c]
        )

    ready = partial.shape[1] // chunk

    def flow_copies(c, done):
        at = pl.ds(c * chunk, chunk)
        some = pl.ds(0, 3 if done else 9)
        copies = [
            pltpu.make_async_copy(density_hbm.at[0, at], density.at[at], flow_sem.at[c, 0]),
            pltpu.make_async_copy(velocity_hbm.at[:, 0, at], velocity.at[:, at], flow_sem.at[c, 1]),
            pltpu.make_async_copy(pressure_hbm.at[0, at], pressure.at[at], flow_sem.at[c, 2]),
            pltpu.make_async_copy(
                metrics_hbm.at[some, 0, at], metrics.at[some, at], flow_sem.at[c, 3]
            ),
        ]
        if done:
            copies.append(
                pltpu.make_async_copy(partial_hbm.at[:, at], partial.at[:, at], flow_sem.at[c, 4])
            )
        return copies

    def out_copy(c):
        at = pl.ds(c * chunk, chunk)
        return pltpu.make_async_copy(out.at[:, at], out_hbm.at[:, 0, at], out_sem.at[c])

    for c in range(bands):
        field_copy(c).start()
    for c in reversed(range(chunks)):
        for copy in flow_copies(c, c < ready):
            copy.start()

    penalty_parts(fields, nx, links, order, received, face_y, face_z, pen_y, pair_z)

    base = 2 * nx

    def scalar(i):
        return table[place, base + i]

    inverse = 1.0 / PIVOT
    near = NEAR * inverse
    far_coef = FAR * inverse

    def band(c, _):
        field_copy(c).wait()
        at = pl.ds(pl.multiple_of(c * rows, rows), rows)

        def load(f, x):
            return f_ref[f, x, at, :].astype(F32)

        def edges(f):
            right_fn = right[f, 1, at, :].astype(F32) + right[f, 2, at, :].astype(F32)
            left_fn = left[f, 1, at, :].astype(F32) + left[f, 2, at, :].astype(F32)
            own_fn = own_left[f, 1, at, :].astype(F32) + own_left[f, 2, at, :].astype(F32)
            right_last = right[f, 0, at, :].astype(F32)
            left_first = left[f, 0, at, :].astype(F32)
            far_plane = far[f, at, :].astype(F32)
            low = (
                scalar(14) * right_fn
                + scalar(4) * load(f, 0)
                + scalar(5) * load(f, 1)
                + scalar(6) * own_fn
                + scalar(7) * left_fn
                + scalar(8) * left_first
                + scalar(11) * far_plane
            )
            high = (
                scalar(15) * left_fn
                + scalar(9) * load(f, nx - 1)
                + scalar(10) * load(f, nx - 2)
                + scalar(12) * far_plane
            )
            return (
                low * inverse,
                (scalar(14) * -far_coef) * right_last,
                (scalar(15) * far_coef) * left_first,
                high * inverse,
            )

        for members in ((0, 1, 2), (3, 4)):
            edge = [edges(f) for f in members]
            state = []
            for q, f in enumerate(members):
                f0, f1, f2, f3 = [load(f, x) for x in range(4)]
                d0 = near * f1 + far_coef * f2 + edge[q][0]
                d1 = near * (f2 - f0) + far_coef * f3 + edge[q][1] - MULT * d0
                line[f, 0, at, :] = d0
                line[f, 1, at, :] = d1
                state.append((f0, f1, f2, f3, d1))

            def forward(x, state):
                new = []
                for q, f in enumerate(members):
                    fm2, fm1, f0, fp1, d = state[q]
                    fp2 = load(f, x + 2)
                    d = (near * (fp1 - fm1) + far_coef * (fp2 - fm2)) - MULT * d
                    line[f, x, at, :] = d
                    new.append((fm1, f0, fp1, fp2, d))
                return tuple(new)

            state = lax.fori_loop(2, nx - 2, forward, tuple(state), unroll=10)
            for q, f in enumerate(members):
                fm2, fm1, f0, fp1, d = state[q]
                d = near * (fp1 - fm1) - far_coef * fm2 + edge[q][2] - MULT * d
                line[f, nx - 2, at, :] = d
                d = -near * f0 - far_coef * fm1 + edge[q][3] - MULT * d
                line[f, nx - 1, at, :] = d
                line[f, nx, at, :] = scalar(13) * d
        return 0

    lax.fori_loop(0, bands, band, 0)

    lane = iota((rows, 256), 1)
    row = iota((BLOCK, nz), 0)

    def matmuls(h, parts, done=False):
        grad_y, grad_z, pens = parts
        mask = (((lane + 1 - 4 * h) & 127) < 4).astype(F32).astype(BF16)
        mask = jnp.concatenate([mask] * (ny // rows), axis=0)

        def along_z_of(f):
            both = f_ref[f, pl.ds(2 * h, 2)].reshape(2 * ny, nz)
            grad_z[f] = dot(jnp.concatenate([both, both], axis=1), along_z[...])

        def pens_of(f):
            got = dot(pair_z[f] * mask, ends[...])
            pens[f, :ny, :] = got[:, :nz]
            pens[f, ny:, :] = got[:, nz:]

        def along_y_of(f):
            wide = jnp.concatenate([f_ref[f, 2 * h], f_ref[f, 2 * h + 1]], axis=1)
            got = dot(along_y[...], jnp.concatenate([wide, wide], axis=0))
            grad_y[f, :ny, :] = got[:, :nz]
            grad_y[f, ny:, :] = got[:, nz:]

        kinds = (pens_of,) if done else (along_z_of, pens_of, along_y_of)
        return [functools.partial(kind, f) for kind in kinds for f in range(fields)]

    def two_cells(h, parts, tasks, done=False):
        grad_y, grad_z, pens = parts
        blocks = 2 * ny // BLOCK
        number = 0
        for q in (1, 0):
            x = 2 * h + q
            for y in range(0, ny, BLOCK):
                number += 1
                for task in tasks[len(tasks) * (number - 1) // blocks : len(tasks) * number // blocks]:
                    task()
                at = slice(y, y + BLOCK)
                here = slice(q * ny + y, q * ny + y + BLOCK)
                rho = density[x, at, :].astype(F32)
                vel = [velocity[i, x, at, :].astype(F32) for i in range(3)]
                press = HEAT * pressure[x, at, :].astype(F32)
                gx = []
                for f in range(fields):
                    value = line[f, x, at, :] - MULT * line[f, x + 1, at, :]
                    line[f, x, at, :] = value
                    gx.append(value)
                grads = [gx]
                if not done:
                    grads.append([grad_y[f, here, :] for f in range(fields)])
                    grads.append([grad_z[f, here, :] for f in range(fields)])
                sums = None
                for d, g in enumerate(grads):
                    metric = [metrics[3 * d + i, x, at, :].astype(F32) for i in range(3)]
                    sums = flux(g, metric, rho, vel, press, sums)
                sums[4] = sums[4] + sums[5] / rho
                for f in range(fields):
                    total = sums[f] + pens[f, here, :]
                    if done:
                        total = total + partial[f, x, at, :]
                    if y == 0:
                        line_y = pen_y[0, pl.ds(f * nx + x, 1), :]
                        total = total + jnp.where(row == 0, line_y, 0.0)
                    if y == ny - BLOCK:
                        line_y = pen_y[1, pl.ds(f * nx + x, 1), :]
                        total = total + jnp.where(row == BLOCK - 1, line_y, 0.0)
                    out[f, x, at, :] = total.astype(BF16)

    now, later = (now_y, now_z, now_p), (later_y, later_z, later_p)
    for task in matmuls(nx // 2 - 1, now):
        task()

    def section(k, _, done=False):
        c = chunks - 1 - k
        for copy in flow_copies(c, done):
            copy.wait()

        def four_cells(i, s):
            h = (c + 1) * (chunk // 2) - 1 - 2 * i
            two_cells(h, now, matmuls(h - 1, later, done), done)
            two_cells(h - 1, later, matmuls(jnp.maximum(h - 2, 0), now, done), done)
            return s

        lax.fori_loop(0, chunk // 4, four_cells, 0, unroll=2)
        out_copy(c).start()
        return 0

    lax.fori_loop(0, chunks - ready, section, 0)
    lax.fori_loop(chunks - ready, chunks, functools.partial(section, done=True), 0)
    for c in range(chunks):
        out_copy(c).wait()


def in_hbm(*arrays):
    return [pltpu.with_memory_space_constraint(a, pltpu.HBM) for a in arrays]


def gather_call(table, order, links, adjoint):
    fields, _, nx, ny, nz = adjoint.shape
    blocks, patches = links.shape[1:]
    lanes = 128 * ((fields + 1) // 2)
    shape = jax.ShapeDtypeStruct
    vmem = pl.BlockSpec(memory_space=pltpu.VMEM)
    return pl.pallas_call(
        functools.partial(gather_kernel, fields),
        in_specs=[pl.BlockSpec(memory_space=pltpu.SMEM)]
        + [pl.BlockSpec(memory_space=pltpu.HBM)] * 3,
        out_specs=[vmem] * 6,
        out_shape=[
            shape((blocks, 16, lanes), BF16),
            shape((fields, 3, ny, nz), BF16),
            shape((fields, 3, ny, nz), BF16),
            shape((fields, ny, nz), BF16),
            shape((fields, nx, 2 * nz), BF16),
            shape((fields, ny, 128), BF16),
        ],
        scratch_shapes=[
            pltpu.VMEM((fields, nx, ny, nz), BF16),
            pltpu.VMEM((nx, 2 * nz), F32),
            pltpu.VMEM((16 * blocks, PW * patches), BF16),
            pltpu.VMEM(links.shape, jnp.int32),
            pltpu.VMEM(order.shape, BF16),
            pltpu.SemaphoreType.DMA((fields,)),
            pltpu.SemaphoreType.DMA((2,)),
        ],
        compiler_params=pltpu.CompilerParams(vmem_limit_bytes=24 * MIB),
        cost_estimate=pl.CostEstimate(flops=10**9, bytes_accessed=7 * 10**6, transcendentals=0),
    )(*in_hbm(table, links, order, adjoint))


def lateral_call(along_y, along_z, adjoint, density, velocity, pressure, metrics):
    fields, _, nx, ny, nz = adjoint.shape
    chunk = LATERAL_CHUNK
    fixed = (lambda i: (0, 0))
    return pl.pallas_call(
        functools.partial(lateral_kernel, fields),
        grid=(READY // chunk,),
        in_specs=[
            pl.BlockSpec(along_y.shape, fixed),
            pl.BlockSpec(along_z.shape, fixed),
            pl.BlockSpec((fields, 1, chunk, ny, nz), lambda i: (0, 0, i, 0, 0)),
            pl.BlockSpec((1, chunk, ny, nz), lambda i: (0, i, 0, 0)),
            pl.BlockSpec((3, 1, chunk, ny, nz), lambda i: (0, 0, i, 0, 0)),
            pl.BlockSpec((1, chunk, ny, nz), lambda i: (0, i, 0, 0)),
            pl.BlockSpec((3, 1, chunk, ny, nz), lambda i: (1, 0, i, 0, 0)),
            pl.BlockSpec((3, 1, chunk, ny, nz), lambda i: (2, 0, i, 0, 0)),
        ],
        out_specs=pl.BlockSpec((fields, chunk, ny, nz), lambda i: (0, i, 0, 0)),
        out_shape=pltpu.HBM((fields, READY, ny, nz), F32),
        compiler_params=pltpu.CompilerParams(vmem_limit_bytes=24 * MIB),
        cost_estimate=pl.CostEstimate(
            flops=10**10, bytes_accessed=27 * 10**6, transcendentals=0
        ),
    )(*in_hbm(along_y, along_z, adjoint, density, velocity, pressure, metrics, metrics))


def main_call(table, order, along_y, along_z, ends, links, flow, partial, edges):
    adjoint = flow[0]
    fields, _, nx, ny, nz = adjoint.shape
    vmem = pl.BlockSpec(memory_space=pltpu.VMEM)
    hbm = pl.BlockSpec(memory_space=pltpu.HBM)
    small = [links, order, along_y, along_z, ends, *edges]
    return pl.pallas_call(
        functools.partial(main_kernel, fields),
        in_specs=[pl.BlockSpec(memory_space=pltpu.SMEM)]
        + [vmem] * len(small)
        + [hbm] * (len(flow) + 1),
        out_specs=hbm,
        out_shape=jax.ShapeDtypeStruct(adjoint.shape, BF16),
        scratch_shapes=[
            pltpu.VMEM((fields, nx, ny, nz), BF16),
            pltpu.VMEM((nx, ny, nz), BF16),
            pltpu.VMEM((3, nx, ny, nz), BF16),
            pltpu.VMEM((nx, ny, nz), BF16),
            pltpu.VMEM((9, nx, ny, nz), BF16),
            pltpu.VMEM(partial.shape, F32),
            pltpu.VMEM((fields, nx, ny, nz), BF16),
            pltpu.VMEM((fields, nx + 1, ny, nz), F32),
            pltpu.VMEM((2, fields * nx, nz), F32),
            pltpu.VMEM((fields, ny, 256), BF16),
            *[pltpu.VMEM((fields, 2 * ny, nz), F32) for _ in range(6)],
            pltpu.SemaphoreType.DMA((ny // 16,)),
            pltpu.SemaphoreType.DMA((nx // 8, 5)),
            pltpu.SemaphoreType.DMA((nx // 8,)),
        ],
        compiler_params=pltpu.CompilerParams(vmem_limit_bytes=52 * MIB),
        cost_estimate=pl.CostEstimate(
            flops=10**10, bytes_accessed=26 * 10**6, transcendentals=0
        ),
    )(*in_hbm(table), *small, *in_hbm(*flow, partial))


def body(tables, adjoint, density, velocity, pressure, metrics, links):
    along_y, along_z, table, order, ends = [jnp.asarray(t) for t in tables]
    send, right, left, far, face_y, face_z = gather_call(table, order, links, adjoint)
    received = lax.all_to_all(send, "blk", 0, 0)
    pieces = lax.axis_size("ax")
    from_left = lax.ppermute(right, "ax", [(i, (i + 1) % pieces) for i in range(pieces)])
    from_right = lax.ppermute(left, "ax", [((i + 1) % pieces, i) for i in range(pieces)])
    from_far = lax.ppermute(far, "ax", [(i, (i + 2) % pieces) for i in range(pieces)])
    flow = (adjoint, density, velocity, pressure, metrics)
    partial = lateral_call(along_y, along_z, *flow)
    edges = (received, from_left, from_right, from_far, left, face_y, face_z)
    return main_call(table, order, along_y, along_z, ends, links, flow, partial, edges)


def solution(mesh):
    in_specs = (
        P(None, "blk", "ax", None, None),
        P("blk", "ax", None, None),
        P(None, "blk", "ax", None, None),
        P("blk", "ax", None, None),
        P(None, "blk", "ax", None, None),
        P(),
    )
    out_specs = P(None, "blk", "ax", None, None)

    def run(*args):
        pieces = mesh.shape["ax"]
        nx, ny, nz = args[0].shape[2:]
        tables = (*lateral_tables(ny, nz), axial_tables(pieces, nx // pieces), lane_order())
        tables = (*tables, end_table(nz))
        return jax.shard_map(
            functools.partial(body, tables),
            mesh=mesh,
            in_specs=in_specs,
            out_specs=out_specs,
            check_vma=False,
        )(*args)

    return run
```
